256 devices in a mesh: sub: 16 (over z, core), sep: 16 (over x, y).
Axes of the slice: x: 4, y: 4, z: 8, core: 2. Of those that a mesh axis runs over, the one named last changes fastest.
Arguments:
- modes: bfloat16 [16, 32768, 1024], P('sub', 'sep'), may hold values from -0.1875 to 0.1875
- coupling: bfloat16 [16, 32768, 512], P('sub', 'sep'), may hold values from -0.046875 to 0.046875
- eigvals: float32 [16, 1024], P('sub'), may hold values from 0.5 to 8
- mode_count: int32 [16], P('sub'), may hold values from 256 to 1024
- sep_map: int32 [16, 4], P('sub'), may hold values from 0 to 31, as said below
- sep_len: int32 [16, 4], P('sub'), may hold values from 64 to 128
- flex: float32 [4096, 4096], P('sep')
- init_vectors: float32 [4096, 256], P('sep'), may hold values from -6 to 6
Outputs:
- separator_modes: float32 [4096, 256], P('sep')
- quotient: float32 [256], replicated
- interior: bfloat16 [16, 32768, 256], P('sub', 'sep')
The draws below stay inside these ranges and needn't reach their ends.
Inputs may be any that keep to these rules, and one draw needn't show every extreme that they name: `sep_map`: each row names 4 different separator blocks.
All inputs are finite; a program needn't handle non-finite values.
Results may differ from the reference program's by a relative error of at most 0.013.
Values may be sent and summed in bfloat16 or wider, within the bound.
No kernel may reach another device: no remote copies, remote signals or barrier semaphores. Data moves between devices by JAX's collectives and lax.ppermute only.
A program may use at most 128 MiB of HBM per device.

```python
import math
import jax
import jax.numpy as jnp
from jax import lax

MODES = 1024
KB = 4
SB = 128
R = 256
ITERS = 2
SUBS = 16
NI = 32768
KSEP = 512
NSB = 32
NS = 4096


def draw_mode_count(key, part):
    key = jax.random.fold_in(key, 11)
    key_a, key_b, key_c = jax.random.split(key, 3)
    counts = jax.random.randint(key_a, (SUBS,), MODES // 4, MODES + 1)
    top_slot = jax.random.randint(key_b, (), 0, SUBS)
    low_slot = (top_slot + 1 + jax.random.randint(key_c, (), 0, SUBS - 1)) % SUBS
    counts = counts.at[top_slot].set(MODES).at[low_slot].set(MODES // 4)
    return counts.astype(jnp.int32)


def draw_sep_map(key, part):
    key = jax.random.fold_in(key, 13)
    key_a, key_b, key_c = jax.random.split(key, 3)
    base_block = jax.random.randint(key_a, (SUBS,), 0, NSB)
    top_slot = jax.random.randint(key_b, (), 0, SUBS)
    low_slot = (top_slot + 1 + jax.random.randint(key_c, (), 0, SUBS - 1)) % SUBS
    base_block = base_block.at[top_slot].set(NSB - 1).at[low_slot].set(0)
    stride = NSB // KB
    return ((base_block[:, None] + jnp.arange(KB, dtype=jnp.int32)[None, :] * stride) % NSB).astype(jnp.int32)


def draw_sep_len(key, part):
    key = jax.random.fold_in(key, 15)
    key_a, key_b, key_c = jax.random.split(key, 3)
    lengths = jax.random.randint(key_a, (SUBS * KB,), SB // 2, SB + 1)
    top_slot = jax.random.randint(key_b, (), 0, SUBS * KB)
    low_slot = (top_slot + 1 + jax.random.randint(key_c, (), 0, SUBS * KB - 1)) % (SUBS * KB)
    lengths = lengths.at[top_slot].set(SB).at[low_slot].set(SB // 2)
    return lengths.reshape(SUBS, KB).astype(jnp.int32)


def draw_flex(key, part):
    key = jax.random.fold_in(key, 17)
    key_a, key_b = jax.random.split(key)
    noise = jax.random.normal(key_a, (NS, NS), jnp.float32)
    diagonal = jax.random.uniform(key_b, (NS,), jnp.float32, 1.0, 4.0)
    identity = jnp.eye(NS, dtype=jnp.float32)
    return (noise * NS ** (-0.5) + identity * diagonal[None, :]).astype(jnp.float32)


def block_levels(rng, shape, pieces, least, high):
    def one(position, shards_of):
        heights = jax.random.uniform(jax.random.fold_in(jax.random.fold_in(rng, 6), position), (shards_of,), jnp.float32, least / len(pieces), high / len(pieces))
        return jnp.repeat(jnp.exp(heights), shape[position] // shards_of).reshape((-1,) + (1,) * (len(shape) - position - 1))

    loudness = one(*pieces[0])
    for cut in pieces[1:]:
        loudness = loudness * one(*cut)
    return loudness


def scatter_about(stream_key, extent, deviation, limit, shards=(), kind=jnp.bfloat16):
    drawn = deviation * jax.random.normal(stream_key, extent, jnp.float32)
    if shards:
        drawn = drawn * block_levels(stream_key, extent, shards, -0.22, 0.18)
    return jnp.clip(drawn, -limit, limit).astype(kind)


def setup_inputs(seed: int = 0) -> dict:
    splits = jax.random.split(jax.random.key(seed), 9)
    modes = scatter_about(splits[0], (SUBS, NI, MODES), MODES ** -0.5, 0.1875, ((0, 16), (1, 16)))
    coupling = scatter_about(splits[1], (SUBS, NI, KSEP), (NI * KSEP // MODES) ** -0.5, 0.046875, ((0, 16), (1, 16)))
    eigvals = jnp.clip(jnp.exp(math.log(8.0) - 2.7725887 * jax.random.uniform(splits[2], (SUBS, MODES), jnp.float32) ** block_levels(splits[2], (SUBS, MODES), ((0, 16),), -0.2, 0.2)), 0.5, 8.0)
    mode_count = draw_mode_count(jax.random.fold_in(splits[8], 71), 0)
    sep_map = draw_sep_map(jax.random.fold_in(splits[8], 71), 0)
    sep_len = draw_sep_len(jax.random.fold_in(splits[8], 71), 0)
    flex = draw_flex(jax.random.fold_in(splits[8], 71), 0)
    init_vectors = scatter_about(splits[7], (NS, R), 1.0, 6.0, ((0, 16),), jnp.float32)
    return dict(modes=modes, coupling=coupling, eigvals=eigvals, mode_count=mode_count, sep_map=sep_map, sep_len=sep_len, flex=flex, init_vectors=init_vectors)


def live_parts(eigvals, mode_count, sep_map, sep_len):
    mode_ids = jnp.arange(MODES, dtype=jnp.int32)
    mode_weight = jnp.where(mode_ids[None, :] < mode_count[:, None], 1.0 / eigvals, 0.0).astype(jnp.float32)
    dof_ids = jnp.arange(SB, dtype=jnp.int32)
    live_dofs = (dof_ids[None, None, :] < sep_len[:, :, None]).reshape(SUBS, KSEP)
    sep_rows = (sep_map[:, :, None] * SB + dof_ids[None, None, :]).reshape(SUBS, KSEP).astype(jnp.int32)
    return (mode_weight, live_dofs, sep_rows)

def reference(modes, coupling, eigvals, mode_count, sep_map, sep_len, flex, init_vectors):
    mode_weight, live_dofs, sep_rows = live_parts(eigvals, mode_count, sep_map, sep_len)

    def project(inputs):
        shapes, couple_rows, live_cols = inputs
        masked = jnp.where(live_cols[None, :], couple_rows, jnp.zeros_like(couple_rows))
        return lax.dot_general(shapes.astype(jnp.float32), masked.astype(jnp.float32), (((0,), (0,)), ((), ())), preferred_element_type=jnp.float32).astype(jnp.bfloat16)
    projected = lax.map(project, (modes, coupling, live_dofs))
    proj_wide = projected.astype(jnp.float32)

    def mode_terms(vectors_bf):
        picked = vectors_bf[sep_rows].astype(jnp.float32)
        amplitude = jnp.einsum('smk,skr->smr', proj_wide, picked)
        return (mode_weight[:, :, None] * amplitude).astype(jnp.bfloat16)
    iterate = init_vectors
    scaling = jnp.sqrt(jnp.float32(NS))
    quotient = jnp.zeros((R,), jnp.float32)
    for sweep_index in range(ITERS):
        vectors_bf = iterate.astype(jnp.bfloat16)
        terms = mode_terms(vectors_bf)
        back_terms = jnp.einsum('smk,smr->skr', proj_wide, terms.astype(jnp.float32))
        coupled = jnp.zeros((NS, R), jnp.float32).at[sep_rows.reshape(-1)].add(back_terms.reshape(SUBS * KSEP, R))
        image = jnp.dot(flex.astype(jnp.float32), vectors_bf.astype(jnp.float32), precision=lax.Precision.HIGHEST, preferred_element_type=jnp.float32) + coupled
        gram = jnp.dot(image.T.astype(jnp.float32), image.astype(jnp.float32), precision=lax.Precision.HIGHEST, preferred_element_type=jnp.float32)
        quotient = lax.optimization_barrier(jnp.sum(iterate * image, axis=0)) / lax.optimization_barrier(jnp.sum(iterate * iterate, axis=0))
        factor = jnp.linalg.cholesky(gram)
        iterate = lax.linalg.triangular_solve(factor, image, left_side=False, lower=True, transpose_a=True) * scaling
    terms = mode_terms(iterate.astype(jnp.bfloat16))

    def expand(inputs):
        shapes, weights_here = inputs
        return jnp.dot(shapes.astype(jnp.float32), weights_here.astype(jnp.float32), preferred_element_type=jnp.float32).astype(jnp.bfloat16)
    interior = lax.map(expand, (modes, terms))
    return (iterate, quotient, interior)
```

```python
import jax
import jax.numpy as jnp
from jax import lax
from jax.experimental import pallas as pl
from jax.experimental.pallas import tpu as pltpu
from jax.sharding import PartitionSpec as P

KB = 4
SB = 128
HIGHEST = lax.Precision.HIGHEST


def dot_f32(a, b, contract=((1,), (0,))):
    return lax.dot_general(
        a, b, (contract, ((), ())), precision=HIGHEST, preferred_element_type=jnp.float32
    )


def inverse_factor_128(block):
    n = block.shape[0]
    lanes = lax.broadcasted_iota(jnp.int32, (8, n), 1)
    subs = lax.broadcasted_iota(jnp.int32, (8, n), 0)
    left = [block[8 * t : 8 * t + 8, :] for t in range(n // 8)]
    right = [jnp.where(lanes == subs + 8 * t, 1.0, 0.0).astype(jnp.float32) for t in range(n // 8)]
    for j in range(n):
        t, r = divmod(j, 8)
        row = left[t][r : r + 1, :]
        inverse_pivot = 1.0 / row[:, j : j + 1]
        row_scaled = row * inverse_pivot
        right_scaled = right[t][r : r + 1, :] * inverse_pivot
        for u in range(t, n // 8):
            column = left[u][:, j : j + 1]
            if u == t:
                if r == 7:
                    continue
                column = jnp.where(subs[:, :1] > r, column, 0.0)
            left[u] = left[u] - column * row_scaled
            right[u] = right[u] - column * right_scaled
    out = []
    for t in range(n // 8):
        pivots = jnp.sum(jnp.where(lanes == subs + 8 * t, left[t], 0.0), axis=1, keepdims=True)
        out.append(right[t] * lax.rsqrt(pivots))
    return jnp.concatenate(out, axis=0)


def factor_kernel(scale, gram_ref, out_ref):
    half = gram_ref.shape[0] // 2
    first = inverse_factor_128(gram_ref[:half, :half])
    below = dot_f32(gram_ref[half:, :half], first, ((1,), (1,)))
    rest = gram_ref[half:, half:] - dot_f32(below, below, ((1,), (1,)))
    second = inverse_factor_128(rest)
    corner = -dot_f32(second, dot_f32(below, first))
    out_ref[:half, :half] = first.T * scale
    out_ref[:half, half:] = corner.T * scale
    out_ref[half:, :half] = jnp.zeros((half, half), jnp.float32)
    out_ref[half:, half:] = second.T * scale


def inverse_transposed_factor(gram, scale):
    return pl.pallas_call(
        lambda gram_ref, out_ref: factor_kernel(scale, gram_ref, out_ref),
        out_shape=jax.ShapeDtypeStruct(gram.shape, jnp.float32),
        in_specs=[pl.BlockSpec(memory_space=pltpu.VMEM)],
        out_specs=pl.BlockSpec(memory_space=pltpu.VMEM),
        cost_estimate=pl.CostEstimate(flops=60_000_000, bytes_accessed=600_000, transcendentals=256),
        name="factor",
    )(gram)


def gather_blocks(x, axis):
    count = lax.axis_size(axis)
    spread = jnp.broadcast_to(x[None], (count,) + x.shape)
    return lax.all_to_all(spread, axis, 0, 0, tiled=True)


def per_device(modes, coupling, eigvals, mode_count, sep_map, sep_len, flex, init_vectors):
    shapes = modes[0]
    sep_count = lax.axis_size("sep")
    sub_count = lax.axis_size("sub")
    sep_index = lax.axis_index("sep")
    sub_index = lax.axis_index("sub")
    layers = sub_count // 2
    layer, core = sub_index // 2, sub_index % 2
    mode_total = shapes.shape[1]
    mode_rows = mode_total // sep_count
    vec_width = init_vectors.shape[1]
    owned_rows = init_vectors.shape[0]
    total_rows = owned_rows * sep_count
    local_dofs = KB * SB
    slim = SB // layers
    scaling = float(total_rows) ** 0.5

    start_vectors = lax.all_gather(init_vectors.astype(jnp.bfloat16), "sep", axis=0, tiled=True)
    map_all = gather_blocks(jnp.pad(sep_map, ((0, 0), (0, 128 - KB))), "sub")[:, 0, :KB]

    dof_ids = jnp.arange(SB, dtype=jnp.int32)
    live_dofs = (dof_ids[None, :] < sep_len[0][:, None]).reshape(1, local_dofs)
    masked = jnp.where(live_dofs, coupling[0], jnp.zeros_like(coupling[0]))
    partial = lax.dot_general(
        shapes, masked, (((0,), (0,)), ((), ())), preferred_element_type=jnp.float32
    )
    shares = lax.all_to_all(
        partial.reshape(sep_count, mode_rows, local_dofs), "sep", 0, 0, tiled=True
    )
    own_projected = jnp.sum(shares, axis=0).astype(jnp.bfloat16)
    projected = gather_blocks(own_projected, "sep").reshape(mode_total, local_dofs)
    mode_ids = jnp.arange(mode_total, dtype=jnp.int32)
    mode_weight = jnp.where(mode_ids < mode_count[0], 1.0 / eigvals[0], 0.0)

    blocks = sep_map[0]
    own_blocks = 2 * sep_index + jnp.arange(2, dtype=jnp.int32)
    picks = own_blocks[:, None] == blocks[None, :]
    by_block = projected.reshape(mode_total, KB, SB)
    picked_columns = jnp.sum(
        jnp.where(picks[None, :, :, None], by_block[:, None], jnp.zeros_like(by_block[:, None])), axis=2
    ).reshape(mode_total, 2 * SB)
    wide = projected.astype(jnp.float32)
    operator_rows = dot_f32(
        picked_columns.astype(jnp.float32), mode_weight[:, None] * wide, ((0,), (0,))
    )
    outgoing = operator_rows.reshape(2, layers, slim, local_dofs).transpose(1, 0, 2, 3)
    incoming = lax.all_to_all(
        outgoing.reshape(sub_count, slim, local_dofs), "sub", 0, 0, tiled=True
    )

    block_total = total_rows // SB
    row_start = core * SB + layer * slim
    flex_rows = lax.dynamic_slice_in_dim(flex, row_start, slim, 0)
    matches = (
        map_all.reshape(-1)[:, None] == jnp.arange(block_total, dtype=jnp.int32)[None, :]
    ).astype(jnp.float32)
    by_source = incoming.reshape(sub_count, slim, KB, SB).transpose(0, 2, 1, 3)
    placed = dot_f32(matches, by_source.reshape(sub_count * KB, slim * SB), ((0,), (0,)))
    operator = flex_rows + placed.reshape(block_total, slim, SB).transpose(1, 0, 2).reshape(
        slim, total_rows
    )
    operator_split = operator.reshape(slim, sep_count, 2, SB).transpose(0, 2, 1, 3).reshape(
        slim, total_rows
    )

    def gather_image(rows):
        part = rows
        for distance in (1, 2, 4):
            perm = [
                (z * 2 + c, (z ^ distance) * 2 + c) for z in range(layers) for c in range(2)
            ]
            other = lax.ppermute(part, "sub", perm)
            upper = (layer & distance) > 0
            part = jnp.where(
                upper,
                jnp.concatenate([other, part], axis=0),
                jnp.concatenate([part, other], axis=0),
            )
        mine = gather_blocks(part, "sep").reshape(total_rows // 2, vec_width)
        theirs = lax.ppermute(mine, "sub", [(i, i ^ 1) for i in range(sub_count)])
        return jnp.concatenate(
            [jnp.where(core == 0, mine, theirs), jnp.where(core == 0, theirs, mine)], axis=0
        )

    def block_at(whole, block):
        place = (block % 2) * sep_count + block // 2
        return lax.dynamic_slice_in_dim(whole, place * SB, SB, 0)

    first_image = gather_image(dot_f32(operator, start_vectors.astype(jnp.float32)))
    second_rows = dot_f32(operator_split, first_image)
    raw_second = gather_image(second_rows)
    first_factor = inverse_transposed_factor(
        dot_f32(first_image, first_image, ((0,), (0,))), scaling
    )
    iterate = dot_f32(first_image, first_factor)
    image = dot_f32(raw_second, first_factor)
    second_factor = inverse_transposed_factor(dot_f32(image, image, ((0,), (0,))), scaling)
    quotient = jnp.sum(iterate * image, axis=0) / jnp.sum(iterate * iterate, axis=0)
    needed = jnp.concatenate(
        [block_at(image, own_blocks[k]) for k in range(2)]
        + [block_at(image, blocks[k]) for k in range(KB)],
        axis=0,
    )
    final = dot_f32(needed, second_factor)
    separator_modes = final[: 2 * SB]
    amplitude = jnp.dot(
        projected, final[2 * SB :].astype(jnp.bfloat16), preferred_element_type=jnp.float32
    )
    terms = (mode_weight[:, None] * amplitude).astype(jnp.bfloat16)
    interior = jnp.dot(shapes, terms, preferred_element_type=jnp.float32)
    return (separator_modes, quotient, interior.astype(jnp.bfloat16)[None])


def solution(mesh):
    placed = (
        P("sub", "sep", None),
        P("sub", "sep", None),
        P("sub", None),
        P("sub"),
        P("sub", None),
        P("sub", None),
        P("sep", None),
        P("sep", None),
    )
    return jax.shard_map(
        per_device,
        mesh=mesh,
        in_specs=placed,
        out_specs=(P("sep", None), P(), P("sub", "sep", None)),
        check_vma=False,
    )
```

```python
import jax
import jax.numpy as jnp
from jax import lax
from jax.experimental import pallas as pl
from jax.experimental.pallas import tpu as pltpu
from jax.sharding import PartitionSpec as P

KB = 4
SB = 128
HIGHEST = lax.Precision.HIGHEST


def dot_f32(a, b, contract=((1,), (0,))):
    return lax.dot_general(
        a, b, (contract, ((), ())), precision=HIGHEST, preferred_element_type=jnp.float32
    )


def inverse_factor_128(block):
    n = block.shape[0]
    lanes = lax.broadcasted_iota(jnp.int32, (8, n), 1)
    subs = lax.broadcasted_iota(jnp.int32, (8, n), 0)
    left = [block[8 * t : 8 * t + 8, :] for t in range(n // 8)]
    right = [jnp.where(lanes == subs + 8 * t, 1.0, 0.0).astype(jnp.float32) for t in range(n // 8)]
    for j in range(n):
        t, r = divmod(j, 8)
        row = left[t][r : r + 1, :]
        inverse_pivot = 1.0 / row[:, j : j + 1]
        row_scaled = row * inverse_pivot
        right_scaled = right[t][r : r + 1, :] * inverse_pivot
        for u in range(t, n // 8):
            column = left[u][:, j : j + 1]
            if u == t:
                if r == 7:
                    continue
                column = jnp.where(subs[:, :1] > r, column, 0.0)
            left[u] = left[u] - column * row_scaled
            right[u] = right[u] - column * right_scaled
    out = []
    for t in range(n // 8):
        pivots = jnp.sum(jnp.where(lanes == subs + 8 * t, left[t], 0.0), axis=1, keepdims=True)
        out.append(right[t] * lax.rsqrt(pivots))
    return jnp.concatenate(out, axis=0)


def factor_kernel(scale, gram_ref, out_ref):
    half = gram_ref.shape[0] // 2
    first = inverse_factor_128(gram_ref[:half, :half])
    below = dot_f32(gram_ref[half:, :half], first, ((1,), (1,)))
    rest = gram_ref[half:, half:] - dot_f32(below, below, ((1,), (1,)))
    second = inverse_factor_128(rest)
    corner = -dot_f32(second, dot_f32(below, first))
    out_ref[:half, :half] = first.T * scale
    out_ref[:half, half:] = corner.T * scale
    out_ref[half:, :half] = jnp.zeros((half, half), jnp.float32)
    out_ref[half:, half:] = second.T * scale


def inverse_transposed_factor(gram, scale, after):
    return pl.pallas_call(
        lambda gram_ref, after_ref, out_ref: factor_kernel(scale, gram_ref, out_ref),
        out_shape=jax.ShapeDtypeStruct(gram.shape, jnp.float32),
        in_specs=[
            pl.BlockSpec(memory_space=pltpu.VMEM),
            pl.BlockSpec(memory_space=pl.ANY),
        ],
        out_specs=pl.BlockSpec(memory_space=pltpu.VMEM),
        cost_estimate=pl.CostEstimate(
            flops=20_000_000_000, bytes_accessed=600_000, transcendentals=256
        ),
        name="factor",
    )(gram, after)


def gather_blocks(x, axis):
    count = lax.axis_size(axis)
    spread = jnp.broadcast_to(x[None], (count,) + x.shape)
    return lax.all_to_all(spread, axis, 0, 0, tiled=True)


def per_device(modes, coupling, eigvals, mode_count, sep_map, sep_len, flex, init_vectors):
    shapes = modes[0]
    sep_count = lax.axis_size("sep")
    sub_count = lax.axis_size("sub")
    sep_index = lax.axis_index("sep")
    sub_index = lax.axis_index("sub")
    layers = sub_count // 2
    layer, core = sub_index // 2, sub_index % 2
    mode_total = shapes.shape[1]
    mode_rows = mode_total // sep_count
    vec_width = init_vectors.shape[1]
    owned_rows = init_vectors.shape[0]
    total_rows = owned_rows * sep_count
    local_dofs = KB * SB
    slim = SB // layers
    scaling = float(total_rows) ** 0.5

    start_vectors = lax.all_gather(init_vectors.astype(jnp.bfloat16), "sep", axis=0, tiled=True)

    dof_ids = jnp.arange(SB, dtype=jnp.int32)
    live_dofs = (dof_ids[None, :] < sep_len[0][:, None]).reshape(1, local_dofs)
    masked = jnp.where(live_dofs, coupling[0], jnp.zeros_like(coupling[0]))
    partial = lax.dot_general(
        shapes, masked, (((0,), (0,)), ((), ())), preferred_element_type=jnp.float32
    )
    shares = lax.all_to_all(
        partial.reshape(sep_count, mode_rows, local_dofs), "sep", 0, 0, tiled=True
    )
    own_projected = jnp.sum(shares, axis=0).astype(jnp.bfloat16)
    projected = gather_blocks(own_projected, "sep").reshape(mode_total, local_dofs)
    mode_ids = jnp.arange(mode_total, dtype=jnp.int32)
    mode_weight = jnp.where(mode_ids < mode_count[0], 1.0 / eigvals[0], 0.0)

    blocks = sep_map[0]
    own_blocks = 2 * sep_index + jnp.arange(2, dtype=jnp.int32)
    picks = own_blocks[:, None] == blocks[None, :]
    by_block = projected.reshape(mode_total, KB, SB)
    picked_columns = jnp.sum(
        jnp.where(picks[None, :, :, None], by_block[:, None], jnp.zeros_like(by_block[:, None])), axis=2
    ).reshape(mode_total, 2 * SB)
    wide = projected.astype(jnp.float32)
    operator_rows = dot_f32(
        picked_columns.astype(jnp.float32), mode_weight[:, None] * wide, ((0,), (0,))
    )
    outgoing = operator_rows.reshape(2, layers, slim, local_dofs).transpose(1, 0, 2, 3)
    outgoing = outgoing.reshape(sub_count, slim, local_dofs)
    map_lanes = jnp.pad(blocks.astype(jnp.float32), (0, SB - KB))
    outgoing = jnp.concatenate(
        [outgoing, jnp.broadcast_to(map_lanes, (sub_count, slim, SB))], axis=2
    )
    incoming = lax.all_to_all(outgoing, "sub", 0, 0, tiled=True)
    map_all = incoming[:, 0, local_dofs : local_dofs + KB].astype(jnp.int32)
    incoming = incoming[:, :, :local_dofs]

    block_total = total_rows // SB
    row_start = core * SB + layer * slim
    flex_rows = lax.dynamic_slice_in_dim(flex, row_start, slim, 0)
    matches = (
        map_all.reshape(-1)[:, None] == jnp.arange(block_total, dtype=jnp.int32)[None, :]
    ).astype(jnp.float32)
    by_source = incoming.reshape(sub_count, slim, KB, SB).transpose(0, 2, 1, 3)
    placed = dot_f32(matches, by_source.reshape(sub_count * KB, slim * SB), ((0,), (0,)))
    operator = flex_rows + placed.reshape(block_total, slim, SB).transpose(1, 0, 2).reshape(
        slim, total_rows
    )
    halves = operator.reshape(slim, sep_count, 2, SB).transpose(2, 0, 1, 3).reshape(
        2, slim, total_rows // 2
    )
    own_half = lax.dynamic_index_in_dim(halves, core, 0, keepdims=False)
    twin_half = lax.dynamic_index_in_dim(halves, 1 - core, 0, keepdims=False)

    def from_twin(x):
        return lax.ppermute(x, "sub", [(i, i ^ 1) for i in range(sub_count)])

    operator_half = jnp.concatenate([own_half, from_twin(twin_half)], axis=0)

    def spread_layers(rows):
        part = rows.reshape(1, 1, 1, slim, vec_width)
        for axis, distance in enumerate((4, 2, 1)):
            perm = [
                (z * 2 + c, (z ^ distance) * 2 + c) for z in range(layers) for c in range(2)
            ]
            other = lax.ppermute(part, "sub", perm)
            upper = (layer & distance) > 0
            part = jnp.where(
                upper,
                jnp.concatenate([other, part], axis=axis),
                jnp.concatenate([part, other], axis=axis),
            )
        return part.reshape(SB, vec_width)

    def gather_half(part):
        return gather_blocks(part, "sep").reshape(total_rows // 2, vec_width)

    first_rows = dot_f32(operator, start_vectors.astype(jnp.float32))
    first_half = gather_half(spread_layers(first_rows))
    both_rows = dot_f32(operator_half, first_half)
    second_rows = both_rows[:slim] + from_twin(both_rows[slim:])
    second_part = spread_layers(second_rows)
    raw_half = gather_half(second_part)

    first_gram = dot_f32(first_half, first_half, ((0,), (0,)))
    first_gram = first_gram + from_twin(first_gram)
    first_factor = inverse_transposed_factor(first_gram, scaling, second_part)
    iterate_half = dot_f32(first_half, first_factor)
    image_half = dot_f32(raw_half, first_factor)
    second_sums = jnp.concatenate(
        [
            dot_f32(image_half, image_half, ((0,), (0,))),
            jnp.sum(iterate_half * image_half, axis=0)[None],
            jnp.sum(iterate_half * iterate_half, axis=0)[None],
            jnp.zeros((6, vec_width), jnp.float32),
        ],
        axis=0,
    )
    second_sums = second_sums + from_twin(second_sums)
    second_factor = inverse_transposed_factor(second_sums[:vec_width], scaling, second_part)
    quotient = second_sums[vec_width] / second_sums[vec_width + 1]
    image_twin = from_twin(image_half)

    def block_at(block):
        here = lax.dynamic_slice_in_dim(image_half, (block // 2) * SB, SB, 0)
        there = lax.dynamic_slice_in_dim(image_twin, (block // 2) * SB, SB, 0)
        return jnp.where(block % 2 == core, here, there)

    needed = jnp.concatenate(
        [block_at(own_blocks[k]) for k in range(2)] + [block_at(blocks[k]) for k in range(KB)],
        axis=0,
    )
    final = dot_f32(needed, second_factor)
    separator_modes = final[: 2 * SB]
    amplitude = jnp.dot(
        projected, final[2 * SB :].astype(jnp.bfloat16), preferred_element_type=jnp.float32
    )
    terms = (mode_weight[:, None] * amplitude).astype(jnp.bfloat16)
    interior = jnp.dot(shapes, terms, preferred_element_type=jnp.float32)
    return (separator_modes, quotient, interior.astype(jnp.bfloat16)[None])


def solution(mesh):
    placed = (
        P("sub", "sep", None),
        P("sub", "sep", None),
        P("sub", None),
        P("sub"),
        P("sub", None),
        P("sub", None),
        P("sep", None),
        P("sep", None),
    )
    return jax.shard_map(
        per_device,
        mesh=mesh,
        in_specs=placed,
        out_specs=(P("sep", None), P(), P("sub", "sep", None)),
        check_vma=False,
    )
```

```python
import jax
import jax.numpy as jnp
from jax import lax
from jax.experimental import pallas as pl
from jax.experimental.pallas import tpu as pltpu
from jax.sharding import PartitionSpec as P

KB = 4
SB = 128
HIGHEST = lax.Precision.HIGHEST


def dot_f32(a, b, contract=((1,), (0,))):
    return lax.dot_general(
        a, b, (contract, ((), ())), precision=HIGHEST, preferred_element_type=jnp.float32
    )


def split_three(x):
    high = x.astype(jnp.bfloat16)
    rest = x - high.astype(jnp.float32)
    middle = rest.astype(jnp.bfloat16)
    return high, middle, (rest - middle.astype(jnp.float32)).astype(jnp.bfloat16)


def invert_factor(left_ref, right_ref):
    n = left_ref.shape[0]
    subs = lax.broadcasted_iota(jnp.int32, (8, n), 0)
    lanes = lax.broadcasted_iota(jnp.int32, (8, n), 1)

    def spread(x, row, lane):
        return jnp.broadcast_to(x[row : row + 1, lane : lane + 1], (8, n))

    def row_of(x, row):
        return jnp.broadcast_to(x[row : row + 1, :], (8, n))

    def stacked(pieces, base):
        out = base
        for row, piece in pieces:
            out = jnp.where(subs == row, piece, out)
        return out

    def panel(t, carry):
        start = pl.multiple_of(8 * t, 8)
        shift = (n - 8 * t) & (n - 1)
        pivots = left_ref[pl.ds(start, 8), :]
        pivots_right = right_ref[pl.ds(start, 8), :]
        corner = pltpu.roll(pivots, shift, 1)
        a = {(i, j): spread(corner, i, j) for i in range(8) for j in range(i + 1)}
        inverse, m = [], {}
        for j in range(8):
            inverse.append(1.0 / a[j, j])
            for i in range(j + 1, 8):
                m[i, j] = a[i, j] * inverse[j]
            for i in range(j + 1, 8):
                for k in range(j + 1, i + 1):
                    a[i, k] = a[i, k] - m[i, j] * a[k, j]
        unit = {}
        for i in range(8):
            for k in range(i):
                total = -m[i, k]
                for j in range(k + 1, i):
                    total = total - m[i, j] * unit[j, k]
                unit[i, k] = total
        zero = jnp.zeros((8, n), jnp.float32)
        down = [stacked([(i, unit[i, k]) for i in range(k + 1, 8)], zero) for k in range(7)]
        up = [stacked([(k, unit[i, k]) for k in range(i)], zero) for i in range(1, 8)]
        scale = stacked([(i, inverse[i]) for i in range(1, 8)], inverse[0])
        root = stacked([(i, a[i, i]) for i in range(1, 8)], a[0, 0])

        def reduce_rows(x):
            for_out = x
            for k in range(7):
                for_out = for_out + down[k] * row_of(x, k)
            scaled = for_out * scale
            back = scaled
            for i in range(1, 8):
                back = back + up[i - 1] * row_of(scaled, i)
            return for_out, back

        _, back_left = reduce_rows(pivots)
        done_right, back_right = reduce_rows(pivots_right)
        heads = jnp.where(lanes > 8 * t + 7, pivots, 0.0)
        upper = split_three(heads)
        lower = split_three(jnp.concatenate([back_left, back_right], axis=1))
        pairs = ((0, 0), (0, 1), (1, 0), (0, 2), (2, 0), (1, 1))
        change = lax.dot_general(
            jnp.concatenate([upper[p] for p, _ in pairs], axis=0),
            jnp.concatenate([lower[q] for _, q in pairs], axis=0),
            (((0,), (0,)), ((), ())),
            preferred_element_type=jnp.float32,
        )
        left_ref[...] = left_ref[...] - change[:, :n]
        right_ref[...] = right_ref[...] - change[:, n:]
        right_ref[pl.ds(start, 8), :] = done_right * lax.rsqrt(root)
        return carry

    lax.fori_loop(0, n // 8, panel, 0)


def factor_kernel(scale, gram_ref, out_ref, left_ref, right_ref):
    half = gram_ref.shape[0] // 2
    identity = jnp.where(
        lax.broadcasted_iota(jnp.int32, (half, half), 0)
        == lax.broadcasted_iota(jnp.int32, (half, half), 1),
        1.0,
        0.0,
    ).astype(jnp.float32)
    left_ref[...] = gram_ref[:half, :half]
    right_ref[...] = identity
    invert_factor(left_ref, right_ref)
    first = right_ref[...]
    below = dot_f32(gram_ref[half:, :half], first, ((1,), (1,)))
    left_ref[...] = gram_ref[half:, half:] - dot_f32(below, below, ((1,), (1,)))
    right_ref[...] = identity
    invert_factor(left_ref, right_ref)
    second = right_ref[...]
    corner = -dot_f32(second, dot_f32(below, first))
    out_ref[:half, :half] = first.T * scale
    out_ref[:half, half:] = corner.T * scale
    out_ref[half:, :half] = jnp.zeros((half, half), jnp.float32)
    out_ref[half:, half:] = second.T * scale


def inverse_transposed_factor(gram, scale, after):
    half = gram.shape[0] // 2
    return pl.pallas_call(
        lambda gram_ref, after_ref, *refs: factor_kernel(scale, gram_ref, *refs),
        out_shape=jax.ShapeDtypeStruct(gram.shape, jnp.float32),
        in_specs=[
            pl.BlockSpec(memory_space=pltpu.VMEM),
            pl.BlockSpec(memory_space=pl.ANY),
        ],
        out_specs=pl.BlockSpec(memory_space=pltpu.VMEM),
        scratch_shapes=[pltpu.VMEM((half, half), jnp.float32)] * 2,
        cost_estimate=pl.CostEstimate(
            flops=12_000_000_000, bytes_accessed=600_000, transcendentals=256
        ),
        name="factor",
    )(gram, after)


def gram_step(x, even_ref, odd_ref):
    high, middle, low = split_three(x)

    def product(a, b):
        return lax.dot_general(
            a, b, (((0,), (0,)), ((), ())), preferred_element_type=jnp.float32
        )

    even_ref[...] += product(high, high) + product(middle, middle)
    odd_ref[...] += product(high, middle) + product(high, low)


def gram_kernel(x_ref, after_ref, out_ref, even_ref, odd_ref):
    @pl.when(pl.program_id(0) == 0)
    def _():
        even_ref[...] = jnp.zeros_like(even_ref)
        odd_ref[...] = jnp.zeros_like(odd_ref)

    gram_step(x_ref[...], even_ref, odd_ref)

    @pl.when(pl.program_id(0) == pl.num_programs(0) - 1)
    def _():
        out_ref[...] = even_ref[...] + odd_ref[...] + odd_ref[...].T


def gram_of(x, after):
    rows, width = x.shape
    step = 256
    return pl.pallas_call(
        gram_kernel,
        grid=(rows // step,),
        out_shape=jax.ShapeDtypeStruct((width, width), jnp.float32),
        in_specs=[
            pl.BlockSpec((step, width), lambda i: (i, 0)),
            pl.BlockSpec(memory_space=pl.ANY),
        ],
        out_specs=pl.BlockSpec((width, width), lambda i: (0, 0)),
        scratch_shapes=[pltpu.VMEM((width, width), jnp.float32)] * 2,
        cost_estimate=pl.CostEstimate(
            flops=3_000_000_000, bytes_accessed=2_400_000, transcendentals=0
        ),
        name="gram",
    )(x, after)


def sums_kernel(raw_ref, iterate_ref, factor_ref, image_ref, out_ref, even_ref, odd_ref, rows_ref):
    @pl.when(pl.program_id(0) == 0)
    def _():
        even_ref[...] = jnp.zeros_like(even_ref)
        odd_ref[...] = jnp.zeros_like(odd_ref)
        rows_ref[...] = jnp.zeros_like(rows_ref)

    image = dot_f32(raw_ref[...], factor_ref[...])
    image_ref[...] = image
    gram_step(image, even_ref, odd_ref)
    iterate = iterate_ref[...]
    rows_ref[0:1, :] += jnp.sum(iterate * image, axis=0, keepdims=True)
    rows_ref[1:2, :] += jnp.sum(iterate * iterate, axis=0, keepdims=True)

    @pl.when(pl.program_id(0) == pl.num_programs(0) - 1)
    def _():
        width = even_ref.shape[0]
        out_ref[:width, :] = even_ref[...] + odd_ref[...] + odd_ref[...].T
        out_ref[width:, :] = rows_ref[...]


def image_and_sums(raw, iterate, factor):
    rows, width = raw.shape
    step = 256
    block = pl.BlockSpec((step, width), lambda i: (i, 0))
    return pl.pallas_call(
        sums_kernel,
        grid=(rows // step,),
        out_shape=(
            jax.ShapeDtypeStruct((rows, width), jnp.float32),
            jax.ShapeDtypeStruct((width + 8, width), jnp.float32),
        ),
        in_specs=[block, block, pl.BlockSpec((width, width), lambda i: (0, 0))],
        out_specs=(block, pl.BlockSpec((width + 8, width), lambda i: (0, 0))),
        scratch_shapes=[
            pltpu.VMEM((width, width), jnp.float32),
            pltpu.VMEM((width, width), jnp.float32),
            pltpu.VMEM((8, width), jnp.float32),
        ],
        cost_estimate=pl.CostEstimate(
            flops=4_000_000_000, bytes_accessed=7_000_000, transcendentals=0
        ),
        name="sums",
    )(raw, iterate, factor)


def final_kernel(place_ref, here_ref, mine_ref, twin_ref, factor_ref, own_ref, touched_ref):
    i = pl.program_id(0)
    image = jnp.where(here_ref[i] == 1, mine_ref[0], twin_ref[0])
    vectors = dot_f32(image, factor_ref[...])

    @pl.when(i < 2)
    def _():
        own_ref[...] = vectors

    @pl.when(i >= 2)
    def _():
        touched_ref[...] = vectors.astype(jnp.bfloat16)


def final_vectors(place, here, mine, twin, factor):
    width = factor.shape[0]
    block = pl.BlockSpec((1, SB, width), lambda i, place, here: (place[i], 0, 0))
    return pl.pallas_call(
        final_kernel,
        grid_spec=pltpu.PrefetchScalarGridSpec(
            num_scalar_prefetch=2,
            grid=(2 + KB,),
            in_specs=[block, block, pl.BlockSpec((width, width), lambda i, place, here: (0, 0))],
            out_specs=(
                pl.BlockSpec((SB, width), lambda i, place, here: (jnp.minimum(i, 1), 0)),
                pl.BlockSpec((SB, width), lambda i, place, here: (jnp.maximum(i - 2, 0), 0)),
            ),
        ),
        out_shape=(
            jax.ShapeDtypeStruct((2 * SB, width), jnp.float32),
            jax.ShapeDtypeStruct((KB * SB, width), jnp.bfloat16),
        ),
        cost_estimate=pl.CostEstimate(
            flops=600_000_000, bytes_accessed=3_000_000, transcendentals=0
        ),
        name="final",
    )(place, here, mine, twin, factor)


def gather_blocks(x, axis):
    count = lax.axis_size(axis)
    spread = jnp.broadcast_to(x[None], (count,) + x.shape)
    return lax.all_to_all(spread, axis, 0, 0, tiled=True)


def per_device(modes, coupling, eigvals, mode_count, sep_map, sep_len, flex, init_vectors):
    shapes = modes[0]
    sep_count = lax.axis_size("sep")
    sub_count = lax.axis_size("sub")
    sep_index = lax.axis_index("sep")
    sub_index = lax.axis_index("sub")
    layers = sub_count // 2
    layer, core = sub_index // 2, sub_index % 2
    mode_total = shapes.shape[1]
    mode_rows = mode_total // sep_count
    vec_width = init_vectors.shape[1]
    owned_rows = init_vectors.shape[0]
    total_rows = owned_rows * sep_count
    local_dofs = KB * SB
    slim = SB // layers
    scaling = float(total_rows) ** 0.5

    def from_twin(x):
        return lax.ppermute(x, "sub", [(i, i ^ 1) for i in range(sub_count)])

    start_rows = lax.dynamic_slice_in_dim(init_vectors, core * SB, SB, 0)
    start_half = lax.all_gather(start_rows.astype(jnp.bfloat16), "sep", axis=0, tiled=True)
    start_twin = from_twin(start_half)

    dof_ids = jnp.arange(SB, dtype=jnp.int32)
    live_dofs = (dof_ids[None, :] < sep_len[0][:, None]).reshape(1, local_dofs)
    masked = jnp.where(live_dofs, coupling[0], jnp.zeros_like(coupling[0]))
    partial = lax.dot_general(
        shapes, masked, (((0,), (0,)), ((), ())), preferred_element_type=jnp.float32
    )
    shares = lax.all_to_all(
        partial.astype(jnp.bfloat16).reshape(sep_count, mode_rows, local_dofs),
        "sep",
        0,
        0,
        tiled=True,
    )
    own_projected = jnp.sum(shares.astype(jnp.float32), axis=0).astype(jnp.bfloat16)
    projected = gather_blocks(own_projected, "sep").reshape(mode_total, local_dofs)
    mode_ids = jnp.arange(mode_total, dtype=jnp.int32)
    mode_weight = jnp.where(mode_ids < mode_count[0], 1.0 / eigvals[0], 0.0)

    blocks = sep_map[0]
    own_blocks = 2 * sep_index + jnp.arange(2, dtype=jnp.int32)
    picks = own_blocks[:, None] == blocks[None, :]
    by_block = projected.reshape(mode_total, KB, SB)
    picked_columns = jnp.sum(
        jnp.where(picks[None, :, :, None], by_block[:, None], jnp.zeros_like(by_block[:, None])), axis=2
    ).reshape(mode_total, 2 * SB)
    wide = projected.astype(jnp.float32)
    operator_rows = dot_f32(
        picked_columns.astype(jnp.float32), mode_weight[:, None] * wide, ((0,), (0,))
    )
    outgoing = operator_rows.reshape(2, layers, slim, local_dofs).transpose(1, 0, 2, 3)
    outgoing = outgoing.reshape(sub_count, slim, local_dofs)
    map_lanes = jnp.pad(blocks.astype(jnp.float32), (0, SB - KB))
    outgoing = jnp.concatenate(
        [outgoing, jnp.broadcast_to(map_lanes, (sub_count, slim, SB))], axis=2
    )
    incoming = lax.all_to_all(outgoing, "sub", 0, 0, tiled=True)
    map_all = incoming[:, 0, local_dofs : local_dofs + KB].astype(jnp.int32)
    incoming = incoming[:, :, :local_dofs]

    block_total = total_rows // SB
    row_start = core * SB + layer * slim
    flex_rows = lax.dynamic_slice_in_dim(flex, row_start, slim, 0)
    matches = (
        map_all.reshape(-1)[:, None] == jnp.arange(block_total, dtype=jnp.int32)[None, :]
    ).astype(jnp.float32)
    by_source = incoming.reshape(sub_count, slim, KB, SB).transpose(0, 2, 1, 3)
    placed = dot_f32(matches, by_source.reshape(sub_count * KB, slim * SB), ((0,), (0,)))
    operator = flex_rows + placed.reshape(block_total, slim, SB).transpose(1, 0, 2).reshape(
        slim, total_rows
    )
    halves = operator.reshape(slim, sep_count, 2, SB).transpose(2, 0, 1, 3).reshape(
        2, slim, total_rows // 2
    )
    own_half = lax.dynamic_index_in_dim(halves, core, 0, keepdims=False)
    twin_half = lax.dynamic_index_in_dim(halves, 1 - core, 0, keepdims=False)

    operator_half = jnp.concatenate([own_half, from_twin(twin_half)], axis=0)

    def spread_layers(rows):
        part = rows.reshape(1, 1, 1, slim, vec_width)
        for axis, distance in enumerate((4, 2, 1)):
            perm = [
                (z * 2 + c, (z ^ distance) * 2 + c) for z in range(layers) for c in range(2)
            ]
            other = lax.ppermute(part, "sub", perm)
            upper = (layer & distance) > 0
            part = jnp.where(
                upper,
                jnp.concatenate([other, part], axis=axis),
                jnp.concatenate([part, other], axis=axis),
            )
        return part.reshape(SB, vec_width)

    def gather_half(part):
        return gather_blocks(part, "sep").reshape(total_rows // 2, vec_width)

    first_rows = dot_f32(
        jnp.concatenate([own_half, twin_half], axis=1),
        jnp.concatenate([start_half, start_twin], axis=0).astype(jnp.float32),
    )
    first_half = gather_half(spread_layers(first_rows))
    both_rows = dot_f32(operator_half, first_half)
    second_rows = both_rows[:slim] + from_twin(both_rows[slim:])
    second_part = spread_layers(second_rows)
    raw_half = gather_half(second_part)

    first_gram = gram_of(first_half, second_part)
    first_gram = first_gram + from_twin(first_gram)
    first_factor = inverse_transposed_factor(first_gram, scaling, second_part)
    iterate_half = dot_f32(first_half, first_factor)

    image_half, second_sums = image_and_sums(raw_half, iterate_half, first_factor)
    second_sums = second_sums + from_twin(second_sums)
    second_factor = inverse_transposed_factor(second_sums[:vec_width], scaling, second_part)
    quotient = second_sums[vec_width] / second_sums[vec_width + 1]
    image_twin = from_twin(image_half)
    wanted = jnp.concatenate([own_blocks, blocks])
    separator_modes, touched = final_vectors(
        wanted // 2,
        (wanted % 2 == core).astype(jnp.int32),
        image_half.reshape(sep_count, SB, vec_width),
        image_twin.reshape(sep_count, SB, vec_width),
        second_factor,
    )
    amplitude = jnp.dot(
        projected, touched, preferred_element_type=jnp.float32
    )
    terms = (mode_weight[:, None] * amplitude).astype(jnp.bfloat16)
    interior = jnp.dot(shapes, terms, preferred_element_type=jnp.float32)
    return (separator_modes, quotient, interior.astype(jnp.bfloat16)[None])


def solution(mesh):
    placed = (
        P("sub", "sep", None),
        P("sub", "sep", None),
        P("sub", None),
        P("sub"),
        P("sub", None),
        P("sub", None),
        P("sep", None),
        P("sep", None),
    )
    return jax.shard_map(
        per_device,
        mesh=mesh,
        in_specs=placed,
        out_specs=(P("sep", None), P(), P("sub", "sep", None)),
        check_vma=False,
    )
```

```python
import jax
import jax.numpy as jnp
from jax import lax
from jax.experimental import pallas as pl
from jax.experimental.pallas import tpu as pltpu
from jax.sharding import PartitionSpec as P

KB = 4
SB = 128
CHUNK = 2048
VMEM_BYTES = 32 * 1024 * 1024
HIGHEST = lax.Precision.HIGHEST
WHOLE = pl.BlockSpec(memory_space=pltpu.VMEM)


def dot_f32(a, b, contract=((1,), (0,))):
    return lax.dot_general(
        a, b, (contract, ((), ())), precision=HIGHEST, preferred_element_type=jnp.float32
    )


def split_three(x):
    high = x.astype(jnp.bfloat16)
    rest = x - high.astype(jnp.float32)
    middle = rest.astype(jnp.bfloat16)
    return high, middle, (rest - middle.astype(jnp.float32)).astype(jnp.bfloat16)


def invert_factor(left_ref, right_ref):
    n = left_ref.shape[0]
    subs = lax.broadcasted_iota(jnp.int32, (8, n), 0)
    lanes = lax.broadcasted_iota(jnp.int32, (8, n), 1)

    def spread(x, row, lane):
        return jnp.broadcast_to(x[row : row + 1, lane : lane + 1], (8, n))

    def row_of(x, row):
        return jnp.broadcast_to(x[row : row + 1, :], (8, n))

    def stacked(pieces, base):
        out = base
        for row, piece in pieces:
            out = jnp.where(subs == row, piece, out)
        return out

    def panel(t, carry):
        start = pl.multiple_of(8 * t, 8)
        shift = (n - 8 * t) & (n - 1)
        pivots = left_ref[pl.ds(start, 8), :]
        pivots_right = right_ref[pl.ds(start, 8), :]
        corner = pltpu.roll(pivots, shift, 1)
        a = {(i, j): spread(corner, i, j) for i in range(8) for j in range(i + 1)}
        inverse, m = [], {}
        for j in range(8):
            inverse.append(1.0 / a[j, j])
            for i in range(j + 1, 8):
                m[i, j] = a[i, j] * inverse[j]
            for i in range(j + 1, 8):
                for k in range(j + 1, i + 1):
                    a[i, k] = a[i, k] - m[i, j] * a[k, j]
        unit = {}
        for i in range(8):
            for k in range(i):
                total = -m[i, k]
                for j in range(k + 1, i):
                    total = total - m[i, j] * unit[j, k]
                unit[i, k] = total
        zero = jnp.zeros((8, n), jnp.float32)
        down = [stacked([(i, unit[i, k]) for i in range(k + 1, 8)], zero) for k in range(7)]
        up = [stacked([(k, unit[i, k]) for k in range(i)], zero) for i in range(1, 8)]
        scale = stacked([(i, inverse[i]) for i in range(1, 8)], inverse[0])
        root = stacked([(i, a[i, i]) for i in range(1, 8)], a[0, 0])

        def reduce_rows(x):
            for_out = x
            for k in range(7):
                for_out = for_out + down[k] * row_of(x, k)
            scaled = for_out * scale
            back = scaled
            for i in range(1, 8):
                back = back + up[i - 1] * row_of(scaled, i)
            return for_out, back

        _, back_left = reduce_rows(pivots)
        done_right, back_right = reduce_rows(pivots_right)
        heads = jnp.where(lanes > 8 * t + 7, pivots, 0.0)
        upper = split_three(heads)
        lower = split_three(jnp.concatenate([back_left, back_right], axis=1))
        pairs = ((0, 0), (0, 1), (1, 0), (0, 2), (2, 0), (1, 1))
        change = lax.dot_general(
            jnp.concatenate([upper[p] for p, _ in pairs], axis=0),
            jnp.concatenate([lower[q] for _, q in pairs], axis=0),
            (((0,), (0,)), ((), ())),
            preferred_element_type=jnp.float32,
        )
        left_ref[...] = left_ref[...] - change[:, :n]
        right_ref[...] = right_ref[...] - change[:, n:]
        right_ref[pl.ds(start, 8), :] = done_right * lax.rsqrt(root)
        return carry

    lax.fori_loop(0, n // 8, panel, 0)


def factor_kernel(scale, gram_ref, twin_ref, out_ref, left_ref, right_ref):
    half = gram_ref.shape[0] // 2
    identity = jnp.where(
        lax.broadcasted_iota(jnp.int32, (half, half), 0)
        == lax.broadcasted_iota(jnp.int32, (half, half), 1),
        1.0,
        0.0,
    ).astype(jnp.float32)
    left_ref[...] = gram_ref[:half, :half] + twin_ref[:half, :half]
    right_ref[...] = identity
    invert_factor(left_ref, right_ref)
    first = right_ref[...]
    below = dot_f32(gram_ref[half:, :half] + twin_ref[half:, :half], first, ((1,), (1,)))
    left_ref[...] = (gram_ref[half:, half:] + twin_ref[half:, half:]) - dot_f32(
        below, below, ((1,), (1,))
    )
    right_ref[...] = identity
    invert_factor(left_ref, right_ref)
    second = right_ref[...]
    corner = -dot_f32(second, dot_f32(below, first))
    out_ref[:half, :half] = first.T * scale
    out_ref[:half, half:] = corner.T * scale
    out_ref[half:, :half] = jnp.zeros((half, half), jnp.float32)
    out_ref[half:, half:] = second.T * scale


def inverse_transposed_factor(gram, twin, scale):
    half = gram.shape[0] // 2
    return pl.pallas_call(
        lambda *refs: factor_kernel(scale, *refs),
        out_shape=jax.ShapeDtypeStruct(gram.shape, jnp.float32),
        in_specs=[pl.BlockSpec(memory_space=pltpu.VMEM)] * 2,
        out_specs=pl.BlockSpec(memory_space=pltpu.VMEM),
        scratch_shapes=[pltpu.VMEM((half, half), jnp.float32)] * 2,
        cost_estimate=pl.CostEstimate(
            flops=12_000_000_000, bytes_accessed=800_000, transcendentals=256
        ),
        name="factor",
    )(gram, twin)


def gram_step(x, even_ref, odd_ref):
    high, middle, low = split_three(x)

    def product(a, b):
        return lax.dot_general(
            a, b, (((0,), (0,)), ((), ())), preferred_element_type=jnp.float32
        )

    even_ref[...] += product(high, high) + product(middle, middle)
    odd_ref[...] += product(high, middle) + product(high, low)


def gram_kernel(x_ref, after_ref, out_ref, even_ref, odd_ref):
    even_ref[...] = jnp.zeros_like(even_ref)
    odd_ref[...] = jnp.zeros_like(odd_ref)

    def chunk(c, carry):
        gram_step(x_ref[pl.ds(pl.multiple_of(c * CHUNK, CHUNK), CHUNK), :], even_ref, odd_ref)
        return carry

    lax.fori_loop(0, x_ref.shape[0] // CHUNK, chunk, 0)
    out_ref[...] = even_ref[...] + odd_ref[...] + odd_ref[...].T


def gram_of(x, after):
    width = x.shape[1]
    return pl.pallas_call(
        gram_kernel,
        out_shape=jax.ShapeDtypeStruct((width, width), jnp.float32),
        in_specs=[WHOLE, pl.BlockSpec(memory_space=pl.ANY)],
        out_specs=WHOLE,
        scratch_shapes=[pltpu.VMEM((width, width), jnp.float32)] * 2,
        compiler_params=pltpu.CompilerParams(vmem_limit_bytes=VMEM_BYTES),
        cost_estimate=pl.CostEstimate(
            flops=2_000_000_000, bytes_accessed=2_400_000, transcendentals=0
        ),
        name="gram",
    )(x, after)


def image_kernel(raw_ref, factor_ref, image_ref, out_ref, even_ref, odd_ref):
    even_ref[...] = jnp.zeros_like(even_ref)
    odd_ref[...] = jnp.zeros_like(odd_ref)

    def chunk(c, carry):
        place = pl.ds(pl.multiple_of(c * CHUNK, CHUNK), CHUNK)
        image = dot_f32(raw_ref[place, :], factor_ref[...])
        image_ref[place, :] = image
        gram_step(image, even_ref, odd_ref)
        return carry

    lax.fori_loop(0, raw_ref.shape[0] // CHUNK, chunk, 0)
    out_ref[...] = even_ref[...] + odd_ref[...] + odd_ref[...].T


def image_and_gram(raw, factor):
    rows, width = raw.shape
    return pl.pallas_call(
        image_kernel,
        out_shape=(
            jax.ShapeDtypeStruct((rows, width), jnp.float32),
            jax.ShapeDtypeStruct((width, width), jnp.float32),
        ),
        in_specs=[WHOLE, WHOLE],
        out_specs=(WHOLE, WHOLE),
        scratch_shapes=[pltpu.VMEM((width, width), jnp.float32)] * 2,
        compiler_params=pltpu.CompilerParams(vmem_limit_bytes=VMEM_BYTES),
        cost_estimate=pl.CostEstimate(
            flops=3_000_000_000, bytes_accessed=5_000_000, transcendentals=0
        ),
        name="image",
    )(raw, factor)


def quotient_kernel(first_ref, factor_ref, image_ref, after_ref, out_ref):
    def chunk(c, carry):
        cross, square = carry
        place = pl.ds(pl.multiple_of(c * CHUNK, CHUNK), CHUNK)
        iterate = dot_f32(first_ref[place, :], factor_ref[...])
        return (
            cross + jnp.sum(iterate * image_ref[place, :], axis=0, keepdims=True),
            square + jnp.sum(iterate * iterate, axis=0, keepdims=True),
        )

    zero = jnp.zeros((1, first_ref.shape[1]), jnp.float32)
    cross, square = lax.fori_loop(0, first_ref.shape[0] // CHUNK, chunk, (zero, zero))
    out_ref[...] = jnp.zeros_like(out_ref)
    out_ref[0:1, :] = cross
    out_ref[1:2, :] = square


def quotient_sums(first, factor, image, after):
    width = first.shape[1]
    return pl.pallas_call(
        quotient_kernel,
        out_shape=jax.ShapeDtypeStruct((8, width), jnp.float32),
        in_specs=[WHOLE, WHOLE, WHOLE, pl.BlockSpec(memory_space=pl.ANY)],
        out_specs=WHOLE,
        compiler_params=pltpu.CompilerParams(vmem_limit_bytes=VMEM_BYTES),
        cost_estimate=pl.CostEstimate(
            flops=2_000_000_000, bytes_accessed=5_000_000, transcendentals=0
        ),
        name="quotient",
    )(first, factor, image, after)


def rows_kernel(blocks_ref, first_ref, weight_ref, gathered_ref, out_ref, start_ref):
    slim = out_ref.shape[1]
    sources, height, modes = gathered_ref.shape
    height = height // 2
    dofs = sources * height
    width = start_ref.shape[2]
    for q in range(modes // width):
        start_ref[:, height * q : height * (q + 1), :] = gathered_ref[
            :, height:, width * q : width * (q + 1)
        ]
    everything = gathered_ref[:, :height, :].reshape(dofs, modes)
    lane = lax.broadcasted_iota(jnp.int32, (slim, SB), 1)
    numbers = jnp.zeros((slim, SB), jnp.int32)
    for k in range(KB):
        numbers = jnp.where(lane == k, blocks_ref[k], numbers)
    numbers = numbers.astype(jnp.float32).astype(jnp.bfloat16)
    for h in range(2):
        wanted = first_ref[0] + h
        place = jnp.int32(0)
        found = jnp.int32(0)
        for k in range(KB):
            hit = (blocks_ref[k] == wanted).astype(jnp.int32)
            place += k * hit
            found += hit
        span = sources // KB
        picked = gathered_ref[pl.ds(place * span, span), :height, :].reshape(SB, modes)
        weighted = picked.astype(jnp.float32) * (weight_ref[...] * found.astype(jnp.float32))
        high, middle, low = split_three(weighted)

        def product(part):
            return lax.dot_general(
                part, everything, (((1,), (1,)), ((), ())), preferred_element_type=jnp.float32
            )

        rows = (product(high) + (product(middle) + product(low))).astype(jnp.bfloat16)
        for z in range(SB // slim):
            out_ref[2 * z + h, :, :dofs] = rows[z * slim : (z + 1) * slim, :]
            out_ref[2 * z + h, :, dofs:] = numbers


def operator_rows(blocks, first, weight, gathered, slim):
    sources, height, modes = gathered.shape
    dofs = sources * height // 2
    width = height * modes // 2 // SB
    scalars = pl.BlockSpec(memory_space=pltpu.SMEM)
    return pl.pallas_call(
        rows_kernel,
        out_shape=(
            jax.ShapeDtypeStruct((2 * SB // slim, slim, dofs + SB), jnp.bfloat16),
            jax.ShapeDtypeStruct((sources, SB, width), jnp.bfloat16),
        ),
        in_specs=[scalars, scalars, WHOLE, WHOLE],
        out_specs=(WHOLE, WHOLE),
        compiler_params=pltpu.CompilerParams(vmem_limit_bytes=VMEM_BYTES),
        cost_estimate=pl.CostEstimate(
            flops=800_000_000, bytes_accessed=2_700_000, transcendentals=0
        ),
        name="rows",
    )(blocks, first, weight, gathered)


def build_kernel(
    map_ref, core_ref, incoming_ref, flex_ref, start_ref, twin_ref,
    rows_ref, own_ref, other_ref, halves_ref,
):
    slim, total = flex_ref.shape
    for b in range(total // SB):
        halves_ref[b % 2, :, (b // 2) * SB : (b // 2 + 1) * SB] = flex_ref[
            :, b * SB : (b + 1) * SB
        ]
    for s in range(incoming_ref.shape[0]):
        for k in range(KB):
            b = map_ref[s * KB + k]
            place = pl.ds(pl.multiple_of((b >> 1) * SB, SB), SB)
            halves_ref[b & 1, :, place] += incoming_ref[s, :, k * SB : (k + 1) * SB].astype(
                jnp.float32
            )
    own = halves_ref[core_ref[0]]
    other = halves_ref[1 - core_ref[0]]
    own_ref[...] = own
    other_ref[...] = other
    first = jnp.dot(
        jnp.concatenate(split_three(own), axis=0), start_ref[...], preferred_element_type=jnp.float32
    )
    second = jnp.dot(
        jnp.concatenate(split_three(other), axis=0), twin_ref[...], preferred_element_type=jnp.float32
    )
    both = first + second
    rows_ref[...] = both[:slim] + (both[slim : 2 * slim] + both[2 * slim :])


def build_rows(map_all, core, incoming, flex, start, twin):
    slim = incoming.shape[1]
    total = flex.shape[1]
    width = start.shape[1]
    scalars = pl.BlockSpec(memory_space=pltpu.SMEM)
    half = jax.ShapeDtypeStruct((slim, total // 2), jnp.float32)
    return pl.pallas_call(
        build_kernel,
        out_shape=(jax.ShapeDtypeStruct((slim, width), jnp.float32), half, half),
        in_specs=[scalars] * 2 + [WHOLE] * 4,
        out_specs=(WHOLE, WHOLE, WHOLE),
        scratch_shapes=[
            pltpu.VMEM((2, slim, total // 2), jnp.float32),
        ],
        compiler_params=pltpu.CompilerParams(vmem_limit_bytes=VMEM_BYTES),
        cost_estimate=pl.CostEstimate(
            flops=300_000_000, bytes_accessed=4_000_000, transcendentals=0
        ),
        name="build",
    )(map_all, core, incoming, flex, start, twin)


def last_kernel(
    scale,
    place_ref, here_ref, gram_ref, gram_twin_ref, mine_ref, twin_ref, weight_ref, gathered_ref,
    modes_ref, own_ref, interior_ref, factor_ref, left_ref, right_ref, image_ref, dofs_ref,
    local_ref, result_ref, image_sems, mode_sem, dofs_sem, result_sems,
):
    count = 2 + KB
    rows = local_ref.shape[0]
    step = rows // 4
    load_modes = pltpu.make_async_copy(modes_ref, local_ref, mode_sem)
    load_dofs = pltpu.make_async_copy(
        gathered_ref.at[:, pl.ds(0, dofs_ref.shape[1]), :], dofs_ref, dofs_sem
    )
    for k in range(count):
        source = pl.ds(pl.multiple_of(place_ref[k] * SB, SB), SB)
        target = image_ref.at[pl.ds(k * SB, SB), :]

        @pl.when(here_ref[k] == 1)
        def _():
            pltpu.make_async_copy(mine_ref.at[source, :], target, image_sems.at[k]).start()

        @pl.when(here_ref[k] != 1)
        def _():
            pltpu.make_async_copy(twin_ref.at[source, :], target, image_sems.at[k]).start()

    load_modes.start()
    load_dofs.start()
    factor_kernel(scale, gram_ref, gram_twin_ref, factor_ref, left_ref, right_ref)
    for k in range(count):
        target = image_ref.at[pl.ds(k * SB, SB), :]
        pltpu.make_async_copy(mine_ref.at[pl.ds(0, SB), :], target, image_sems.at[k]).wait()
    load_dofs.wait()
    load_modes.wait()
    vectors = dot_f32(image_ref[...], factor_ref[...])
    own_ref[...] = vectors[: 2 * SB, :]
    touched = vectors[2 * SB :, :].astype(jnp.bfloat16)
    amplitude = lax.dot_general(
        touched,
        dofs_ref[...].reshape(KB * SB, dofs_ref.shape[2]),
        (((0,), (0,)), ((), ())),
        preferred_element_type=jnp.float32,
    )
    terms = (weight_ref[...] * amplitude).astype(jnp.bfloat16)
    stores = []
    for c in range(4):
        part = pl.ds(c * step, step)
        result_ref[part, :] = lax.dot_general(
            local_ref[part, :], terms, (((1,), (1,)), ((), ())), preferred_element_type=jnp.float32
        ).astype(jnp.bfloat16)
        stores.append(
            pltpu.make_async_copy(result_ref.at[part, :], interior_ref.at[part, :], result_sems.at[c])
        )
        stores[-1].start()
    for store in stores:
        store.wait()


def last_products(place, here, gram, gram_twin, mine, twin, weight, gathered, modes, scale):
    width = gram.shape[0]
    rows, count = modes.shape
    scalars = pl.BlockSpec(memory_space=pltpu.SMEM)
    anywhere = pl.BlockSpec(memory_space=pl.ANY)
    return pl.pallas_call(
        lambda *refs: last_kernel(scale, *refs),
        in_specs=[scalars, scalars, WHOLE, WHOLE, anywhere, anywhere, WHOLE, anywhere, anywhere],
        out_specs=(WHOLE, anywhere),
        out_shape=(
            jax.ShapeDtypeStruct((2 * SB, width), jnp.float32),
            jax.ShapeDtypeStruct((rows, width), jnp.bfloat16),
        ),
        scratch_shapes=[
            pltpu.VMEM((width, width), jnp.float32),
            pltpu.VMEM((width // 2, width // 2), jnp.float32),
            pltpu.VMEM((width // 2, width // 2), jnp.float32),
            pltpu.VMEM(((2 + KB) * SB, width), jnp.float32),
            pltpu.VMEM((gathered.shape[0], gathered.shape[1] // 2, count), jnp.bfloat16),
            pltpu.VMEM((rows, count), jnp.bfloat16),
            pltpu.VMEM((rows, width), jnp.bfloat16),
            pltpu.SemaphoreType.DMA((2 + KB,)),
            pltpu.SemaphoreType.DMA,
            pltpu.SemaphoreType.DMA,
            pltpu.SemaphoreType.DMA((4,)),
        ],
        compiler_params=pltpu.CompilerParams(vmem_limit_bytes=VMEM_BYTES),
        cost_estimate=pl.CostEstimate(
            flops=16_000_000_000, bytes_accessed=8_000_000, transcendentals=256
        ),
        name="last",
    )(place, here, gram, gram_twin, mine, twin, weight, gathered, modes)


def gather_blocks(x, axis):
    count = lax.axis_size(axis)
    spread = jnp.broadcast_to(x[None], (count,) + x.shape)
    return lax.all_to_all(spread, axis, 0, 0, tiled=True)


def per_device(modes, coupling, eigvals, mode_count, sep_map, sep_len, flex, init_vectors):
    shapes = modes[0]
    sep_count = lax.axis_size("sep")
    sub_count = lax.axis_size("sub")
    sep_index = lax.axis_index("sep")
    sub_index = lax.axis_index("sub")
    layers = sub_count // 2
    layer, core = sub_index >> 1, sub_index & 1
    mode_total = shapes.shape[1]
    vec_width = init_vectors.shape[1]
    owned_rows = init_vectors.shape[0]
    total_rows = owned_rows * sep_count
    local_dofs = KB * SB
    slim = SB // layers
    scaling = float(total_rows) ** 0.5

    def from_twin(x):
        return lax.ppermute(x, "sub", [(i, i ^ 1) for i in range(sub_count)])

    dof_ids = jnp.arange(SB, dtype=jnp.int32)
    live_dofs = (dof_ids[None, :] < sep_len[0][:, None]).reshape(local_dofs, 1)
    partial = lax.dot_general(
        coupling[0], shapes, (((0,), (0,)), ((), ())), preferred_element_type=jnp.float32
    )
    partial = jnp.where(live_dofs, partial, 0.0).astype(jnp.bfloat16)
    shares = lax.all_to_all(
        partial.reshape(sep_count, local_dofs // sep_count, mode_total), "sep", 0, 0, tiled=True
    )
    own_projected = jnp.sum(shares.astype(jnp.float32), axis=0).astype(jnp.bfloat16)
    share = local_dofs // sep_count
    fold = mode_total // vec_width
    start_rows = lax.dynamic_slice_in_dim(init_vectors, core * SB, SB, 0).astype(jnp.bfloat16)
    start_rows = jnp.concatenate([start_rows[share * q : share * (q + 1)] for q in range(fold)], axis=1)
    gathered = gather_blocks(jnp.concatenate([own_projected, start_rows], axis=0), "sep")
    mode_ids = jnp.arange(mode_total, dtype=jnp.int32)[None]
    mode_weight = jnp.where(mode_ids < mode_count[0], 1.0 / eigvals, 0.0)

    blocks = sep_map[0]
    outgoing, start_half = operator_rows(
        blocks, (2 * sep_index)[None], mode_weight, gathered, slim
    )
    start_half = start_half.reshape(total_rows // 2, vec_width)
    start_twin = from_twin(start_half)
    incoming = lax.all_to_all(outgoing, "sub", 0, 0, tiled=True)
    map_all = incoming[:, 0, local_dofs : local_dofs + KB].astype(jnp.int32).reshape(-1)

    row_start = core * SB + layer * slim
    flex_rows = lax.dynamic_slice_in_dim(flex, row_start, slim, 0)
    first_rows, own_half, twin_half = build_rows(
        map_all, core[None], incoming, flex_rows, start_half, start_twin
    )
    operator_half = jnp.concatenate([own_half, from_twin(twin_half)], axis=0)

    def from_layer(x, distance):
        perm = [(z * 2 + c, (z ^ distance) * 2 + c) for z in range(layers) for c in range(2)]
        return lax.ppermute(x, "sub", perm)

    def spread_layers(rows):
        other = from_layer(rows, 4)
        upper = (layer & 4) > 0
        pair = jnp.stack([jnp.where(upper, other, rows), jnp.where(upper, rows, other)])
        pieces = [pair] + [from_layer(pair, distance) for distance in (1, 2, 3)]
        odd, high = (layer & 1) > 0, (layer & 2) > 0
        pieces = [jnp.where(odd, pieces[q ^ 1], pieces[q]) for q in range(4)]
        pieces = [jnp.where(high, pieces[q ^ 2], pieces[q]) for q in range(4)]
        return jnp.stack(pieces, axis=1).reshape(SB, vec_width)

    def gather_half(part):
        return gather_blocks(part, "sep").reshape(total_rows // 2, vec_width)

    first_half = gather_half(spread_layers(first_rows))
    both_rows = dot_f32(operator_half, first_half)
    second_rows = both_rows[:slim] + from_twin(both_rows[slim:])
    second_part = spread_layers(second_rows)
    raw_half = gather_half(second_part)

    first_gram = gram_of(first_half, second_part)
    first_factor = inverse_transposed_factor(first_gram, from_twin(first_gram), scaling)

    image_half, second_gram = image_and_gram(raw_half, first_factor)
    sums = quotient_sums(first_half, first_factor, image_half, second_gram)
    sums = sums + from_twin(sums)
    quotient = sums[0] / sums[1]
    wanted = jnp.concatenate([2 * sep_index + jnp.arange(2, dtype=jnp.int32), blocks])
    separator_modes, interior = last_products(
        wanted >> 1,
        ((wanted & 1) == core).astype(jnp.int32),
        second_gram,
        from_twin(second_gram),
        image_half,
        from_twin(image_half),
        mode_weight,
        gathered,
        shapes,
        scaling,
    )
    return (separator_modes, quotient, interior[None])


def solution(mesh):
    placed = (
        P("sub", "sep", None),
        P("sub", "sep", None),
        P("sub", None),
        P("sub"),
        P("sub", None),
        P("sub", None),
        P("sep", None),
        P("sep", None),
    )
    return jax.shard_map(
        per_device,
        mesh=mesh,
        in_specs=placed,
        out_specs=(P("sep", None), P(), P("sub", "sep", None)),
        check_vma=False,
    )
```

```python
import jax
import jax.numpy as jnp
from jax import lax
from jax.experimental import pallas as pl
from jax.experimental.pallas import tpu as pltpu
from jax.sharding import PartitionSpec as P

KB = 4
SB = 128
CHUNK = 2048
VMEM_BYTES = 20 * 1024 * 1024
HIGHEST = lax.Precision.HIGHEST
WHOLE = pl.BlockSpec(memory_space=pltpu.VMEM)


def dot_f32(a, b, contract=((1,), (0,))):
    return lax.dot_general(
        a, b, (contract, ((), ())), precision=HIGHEST, preferred_element_type=jnp.float32
    )


def split_three(x):
    high = x.astype(jnp.bfloat16)
    rest = x - high.astype(jnp.float32)
    middle = rest.astype(jnp.bfloat16)
    return high, middle, (rest - middle.astype(jnp.float32)).astype(jnp.bfloat16)


def invert_factor(left_ref, right_ref):
    n = left_ref.shape[0]
    subs = lax.broadcasted_iota(jnp.int32, (8, n), 0)
    lanes = lax.broadcasted_iota(jnp.int32, (8, n), 1)

    def spread(x, row, lane):
        return jnp.broadcast_to(x[row : row + 1, lane : lane + 1], (8, n))

    def row_of(x, row):
        return jnp.broadcast_to(x[row : row + 1, :], (8, n))

    def stacked(pieces, base):
        out = base
        for row, piece in pieces:
            out = jnp.where(subs == row, piece, out)
        return out

    def panel(t, carry):
        start = pl.multiple_of(8 * t, 8)
        shift = (n - 8 * t) & (n - 1)
        pivots = left_ref[pl.ds(start, 8), :]
        pivots_right = right_ref[pl.ds(start, 8), :]
        corner = pltpu.roll(pivots, shift, 1)
        a = {(i, j): spread(corner, i, j) for i in range(8) for j in range(i + 1)}
        inverse, m = [], {}
        for j in range(8):
            inverse.append(1.0 / a[j, j])
            for i in range(j + 1, 8):
                m[i, j] = a[i, j] * inverse[j]
            for i in range(j + 1, 8):
                for k in range(j + 1, i + 1):
                    a[i, k] = a[i, k] - m[i, j] * a[k, j]
        unit = {}
        for i in range(8):
            for k in range(i):
                total = -m[i, k]
                for j in range(k + 1, i):
                    total = total - m[i, j] * unit[j, k]
                unit[i, k] = total
        zero = jnp.zeros((8, n), jnp.float32)
        down = [stacked([(i, unit[i, k]) for i in range(k + 1, 8)], zero) for k in range(7)]
        up = [stacked([(k, unit[i, k]) for k in range(i)], zero) for i in range(1, 8)]
        scale = stacked([(i, inverse[i]) for i in range(1, 8)], inverse[0])
        root = stacked([(i, a[i, i]) for i in range(1, 8)], a[0, 0])

        def reduce_rows(x):
            for_out = x
            for k in range(7):
                for_out = for_out + down[k] * row_of(x, k)
            scaled = for_out * scale
            back = scaled
            for i in range(1, 8):
                back = back + up[i - 1] * row_of(scaled, i)
            return for_out, back

        _, back_left = reduce_rows(pivots)
        done_right, back_right = reduce_rows(pivots_right)
        heads = jnp.where(lanes > 8 * t + 7, pivots, 0.0)
        upper = split_three(heads)
        lower = split_three(jnp.concatenate([back_left, back_right], axis=1))
        pairs = ((0, 0), (0, 1), (1, 0), (0, 2), (2, 0), (1, 1))
        change = lax.dot_general(
            jnp.concatenate([upper[p] for p, _ in pairs], axis=0),
            jnp.concatenate([lower[q] for _, q in pairs], axis=0),
            (((0,), (0,)), ((), ())),
            preferred_element_type=jnp.float32,
        )
        left_ref[...] = left_ref[...] - change[:, :n]
        right_ref[...] = right_ref[...] - change[:, n:]
        right_ref[pl.ds(start, 8), :] = done_right * lax.rsqrt(root)
        return carry

    lax.fori_loop(0, n // 8, panel, 0)


def factor_kernel(scale, gram_ref, twin_ref, out_ref, left_ref, right_ref):
    half = gram_ref.shape[1] // 2
    identity = jnp.where(
        lax.broadcasted_iota(jnp.int32, (half, half), 0)
        == lax.broadcasted_iota(jnp.int32, (half, half), 1),
        1.0,
        0.0,
    ).astype(jnp.float32)
    left_ref[...] = gram_ref[:half, :half] + twin_ref[:half, :half]
    right_ref[...] = identity
    invert_factor(left_ref, right_ref)
    first = right_ref[...]
    below = dot_f32(gram_ref[half : 2 * half, :half] + twin_ref[half : 2 * half, :half], first, ((1,), (1,)))
    left_ref[...] = (
        gram_ref[half : 2 * half, half:] + twin_ref[half : 2 * half, half:]
    ) - dot_f32(below, below, ((1,), (1,)))
    right_ref[...] = identity
    invert_factor(left_ref, right_ref)
    second = right_ref[...]
    corner = -dot_f32(second, dot_f32(below, first))
    out_ref[:half, :half] = first.T * scale
    out_ref[:half, half:] = corner.T * scale
    out_ref[half:, :half] = jnp.zeros((half, half), jnp.float32)
    out_ref[half:, half:] = second.T * scale


def inverse_transposed_factor(gram, twin, scale):
    half = gram.shape[0] // 2
    return pl.pallas_call(
        lambda *refs: factor_kernel(scale, *refs),
        out_shape=jax.ShapeDtypeStruct(gram.shape, jnp.float32),
        in_specs=[pl.BlockSpec(memory_space=pltpu.VMEM)] * 2,
        out_specs=pl.BlockSpec(memory_space=pltpu.VMEM),
        scratch_shapes=[pltpu.VMEM((half, half), jnp.float32)] * 2,
        compiler_params=pltpu.CompilerParams(vmem_limit_bytes=VMEM_BYTES),
        cost_estimate=pl.CostEstimate(
            flops=12_000_000_000, bytes_accessed=800_000, transcendentals=256
        ),
        name="factor",
    )(gram, twin)


def gram_step(x, even_ref, odd_ref):
    high, middle, low = split_three(x)

    def product(a, b):
        return lax.dot_general(
            a, b, (((0,), (0,)), ((), ())), preferred_element_type=jnp.float32
        )

    even_ref[...] += product(high, high) + product(middle, middle)
    odd_ref[...] += product(high, middle) + product(high, low)


def gram_kernel(x_ref, after_ref, out_ref, even_ref, odd_ref):
    even_ref[...] = jnp.zeros_like(even_ref)
    odd_ref[...] = jnp.zeros_like(odd_ref)

    def chunk(c, carry):
        gram_step(x_ref[pl.ds(pl.multiple_of(c * CHUNK, CHUNK), CHUNK), :], even_ref, odd_ref)
        return carry

    lax.fori_loop(0, x_ref.shape[0] // CHUNK, chunk, 0)
    out_ref[...] = even_ref[...] + odd_ref[...] + odd_ref[...].T


def gram_of(x, after):
    width = x.shape[1]
    return pl.pallas_call(
        gram_kernel,
        out_shape=jax.ShapeDtypeStruct((width, width), jnp.float32),
        in_specs=[WHOLE, pl.BlockSpec(memory_space=pl.ANY)],
        out_specs=WHOLE,
        scratch_shapes=[pltpu.VMEM((width, width), jnp.float32)] * 2,
        compiler_params=pltpu.CompilerParams(vmem_limit_bytes=VMEM_BYTES),
        cost_estimate=pl.CostEstimate(
            flops=2_000_000_000, bytes_accessed=2_400_000, transcendentals=0
        ),
        name="gram",
    )(x, after)


def iterate_kernel(first_ref, factor_ref, iterate_ref):
    iterate_ref[...] = dot_f32(first_ref[...], factor_ref[...])


def iterate_of(first, factor):
    return pl.pallas_call(
        iterate_kernel,
        out_shape=jax.ShapeDtypeStruct(first.shape, jnp.float32),
        in_specs=[WHOLE, WHOLE],
        out_specs=WHOLE,
        compiler_params=pltpu.CompilerParams(vmem_limit_bytes=VMEM_BYTES),
        cost_estimate=pl.CostEstimate(
            flops=2_000_000_000, bytes_accessed=4_000_000, transcendentals=0
        ),
        name="iterate",
    )(first, factor)


def image_kernel(raw_ref, iterate_ref, factor_ref, image_ref, out_ref, even_ref, odd_ref):
    width = even_ref.shape[0]
    even_ref[...] = jnp.zeros_like(even_ref)
    odd_ref[...] = jnp.zeros_like(odd_ref)
    image = dot_f32(raw_ref[...], factor_ref[...])
    image_ref[...] = image
    gram_step(image, even_ref, odd_ref)
    iterate = iterate_ref[...]
    out_ref[width:, :] = jnp.zeros((out_ref.shape[0] - width, width), jnp.float32)
    out_ref[width : width + 1, :] = jnp.sum(iterate * image, axis=0, keepdims=True)
    out_ref[width + 1 : width + 2, :] = jnp.sum(iterate * iterate, axis=0, keepdims=True)
    out_ref[:width, :] = even_ref[...] + odd_ref[...] + odd_ref[...].T


def image_and_sums(raw, iterate, factor):
    rows, width = raw.shape
    return pl.pallas_call(
        image_kernel,
        out_shape=(
            jax.ShapeDtypeStruct((rows, width), jnp.float32),
            jax.ShapeDtypeStruct((width + 8, width), jnp.float32),
        ),
        in_specs=[WHOLE, WHOLE, WHOLE],
        out_specs=(WHOLE, WHOLE),
        scratch_shapes=[pltpu.VMEM((width, width), jnp.float32)] * 2,
        compiler_params=pltpu.CompilerParams(vmem_limit_bytes=VMEM_BYTES),
        cost_estimate=pl.CostEstimate(
            flops=3_000_000_000, bytes_accessed=7_000_000, transcendentals=0
        ),
        name="image",
    )(raw, iterate, factor)


def spread_kernel(low_ref, own_ref, one_ref, two_ref, three_ref, after_ref, out_ref, part_ref, sems):
    slim = own_ref.shape[1]
    for e, piece_ref in enumerate((own_ref, one_ref, two_ref, three_ref)):
        for b in range(2):
            place = (4 * b + (low_ref[0] ^ e)) * slim
            part_ref[pl.ds(pl.multiple_of(place, slim), slim), :] = piece_ref[b]
    copies = [
        pltpu.make_async_copy(part_ref, out_ref.at[k], sems.at[k]) for k in range(out_ref.shape[0])
    ]
    for copy in copies:
        copy.start()
    for copy in copies:
        copy.wait()


def spread_rows(low, pieces, after, count):
    slim, width = pieces[0].shape[1:]
    anywhere = pl.BlockSpec(memory_space=pl.ANY)
    return pl.pallas_call(
        spread_kernel,
        out_shape=jax.ShapeDtypeStruct((count, 8 * slim, width), jnp.float32),
        in_specs=[pl.BlockSpec(memory_space=pltpu.SMEM)] + [WHOLE] * 4 + [anywhere],
        out_specs=anywhere,
        scratch_shapes=[
            pltpu.VMEM((8 * slim, width), jnp.float32),
            pltpu.SemaphoreType.DMA((count,)),
        ],
        cost_estimate=pl.CostEstimate(flops=0, bytes_accessed=2_400_000, transcendentals=0),
        name="spread",
    )(low, *pieces, after)


def rows_kernel(blocks_ref, first_ref, weight_ref, gathered_ref, out_ref, start_ref):
    slim = out_ref.shape[1]
    sources, height, modes = gathered_ref.shape
    height = height // 2
    dofs = sources * height
    width = start_ref.shape[2]
    for q in range(modes // width):
        start_ref[:, height * q : height * (q + 1), :] = gathered_ref[
            :, height:, width * q : width * (q + 1)
        ]
    everything = gathered_ref[:, :height, :].reshape(dofs, modes)
    lane = lax.broadcasted_iota(jnp.int32, (slim, SB), 1)
    numbers = jnp.zeros((slim, SB), jnp.int32)
    for k in range(KB):
        numbers = jnp.where(lane == k, blocks_ref[k], numbers)
    numbers = numbers.astype(jnp.float32).astype(jnp.bfloat16)
    for h in range(2):
        wanted = first_ref[0] + h
        place = jnp.int32(0)
        found = jnp.int32(0)
        for k in range(KB):
            hit = (blocks_ref[k] == wanted).astype(jnp.int32)
            place += k * hit
            found += hit
        span = sources // KB
        picked = gathered_ref[pl.ds(place * span, span), :height, :].reshape(SB, modes)
        weighted = picked.astype(jnp.float32) * (weight_ref[...] * found.astype(jnp.float32))
        high, middle, low = split_three(weighted)

        def product(part):
            return lax.dot_general(
                part, everything, (((1,), (1,)), ((), ())), preferred_element_type=jnp.float32
            )

        rows = (product(high) + (product(middle) + product(low))).astype(jnp.bfloat16)
        for z in range(SB // slim):
            out_ref[2 * z + h, :, :dofs] = rows[z * slim : (z + 1) * slim, :]
            out_ref[2 * z + h, :, dofs:] = numbers


def operator_rows(blocks, first, weight, gathered, slim):
    sources, height, modes = gathered.shape
    dofs = sources * height // 2
    width = height * modes // 2 // SB
    scalars = pl.BlockSpec(memory_space=pltpu.SMEM)
    return pl.pallas_call(
        rows_kernel,
        out_shape=(
            jax.ShapeDtypeStruct((2 * SB // slim, slim, dofs + SB), jnp.bfloat16),
            jax.ShapeDtypeStruct((sources, SB, width), jnp.bfloat16),
        ),
        in_specs=[scalars, scalars, WHOLE, WHOLE],
        out_specs=(WHOLE, WHOLE),
        compiler_params=pltpu.CompilerParams(vmem_limit_bytes=VMEM_BYTES),
        cost_estimate=pl.CostEstimate(
            flops=800_000_000, bytes_accessed=2_700_000, transcendentals=0
        ),
        name="rows",
    )(blocks, first, weight, gathered)


def build_kernel(
    map_ref, core_ref, incoming_ref, flex_ref, start_ref, twin_ref,
    rows_ref, own_ref, other_ref, halves_ref,
):
    slim, total = flex_ref.shape
    for b in range(total // SB):
        halves_ref[b % 2, :, (b // 2) * SB : (b // 2 + 1) * SB] = flex_ref[
            :, b * SB : (b + 1) * SB
        ]
    for s in range(incoming_ref.shape[0]):
        for k in range(KB):
            b = map_ref[s * KB + k]
            place = pl.ds(pl.multiple_of((b >> 1) * SB, SB), SB)
            halves_ref[b & 1, :, place] += incoming_ref[s, :, k * SB : (k + 1) * SB].astype(
                jnp.float32
            )
    own = halves_ref[core_ref[0]]
    other = halves_ref[1 - core_ref[0]]
    own_ref[...] = own
    other_ref[...] = other
    first = jnp.dot(
        jnp.concatenate(split_three(own), axis=0), start_ref[...], preferred_element_type=jnp.float32
    )
    second = jnp.dot(
        jnp.concatenate(split_three(other), axis=0), twin_ref[...], preferred_element_type=jnp.float32
    )
    both = first + second
    rows_ref[...] = both[:slim] + (both[slim : 2 * slim] + both[2 * slim :])


def build_rows(map_all, core, incoming, flex, start, twin):
    slim = incoming.shape[1]
    total = flex.shape[1]
    width = start.shape[1]
    scalars = pl.BlockSpec(memory_space=pltpu.SMEM)
    half = jax.ShapeDtypeStruct((slim, total // 2), jnp.float32)
    return pl.pallas_call(
        build_kernel,
        out_shape=(jax.ShapeDtypeStruct((slim, width), jnp.float32), half, half),
        in_specs=[scalars] * 2 + [WHOLE] * 4,
        out_specs=(WHOLE, WHOLE, WHOLE),
        scratch_shapes=[
            pltpu.VMEM((2, slim, total // 2), jnp.float32),
        ],
        compiler_params=pltpu.CompilerParams(vmem_limit_bytes=VMEM_BYTES),
        cost_estimate=pl.CostEstimate(
            flops=300_000_000, bytes_accessed=4_000_000, transcendentals=0
        ),
        name="build",
    )(map_all, core, incoming, flex, start, twin)


def last_kernel(
    scale,
    place_ref, here_ref, gram_ref, gram_twin_ref, mine_ref, twin_ref, weight_ref, gathered_ref,
    modes_ref, own_ref, quotient_ref, interior_ref, factor_ref, left_ref, right_ref, image_ref, dofs_ref,
    local_ref, result_ref, image_sems, mode_sem, dofs_sem, result_sems,
):
    count = 2 + KB
    rows = local_ref.shape[0]
    step = rows // 4
    load_modes = pltpu.make_async_copy(modes_ref, local_ref, mode_sem)
    load_dofs = pltpu.make_async_copy(
        gathered_ref.at[:, pl.ds(0, dofs_ref.shape[1]), :], dofs_ref, dofs_sem
    )
    for k in range(count):
        source = pl.ds(pl.multiple_of(place_ref[k] * SB, SB), SB)
        target = image_ref.at[pl.ds(k * SB, SB), :]

        @pl.when(here_ref[k] == 1)
        def _():
            pltpu.make_async_copy(mine_ref.at[source, :], target, image_sems.at[k]).start()

        @pl.when(here_ref[k] != 1)
        def _():
            pltpu.make_async_copy(twin_ref.at[source, :], target, image_sems.at[k]).start()

    load_modes.start()
    load_dofs.start()
    width = gram_ref.shape[1]
    sums = gram_ref[width:, :] + gram_twin_ref[width:, :]
    quotient_ref[...] = sums[0:1, :] / sums[1:2, :]
    factor_kernel(scale, gram_ref, gram_twin_ref, factor_ref, left_ref, right_ref)
    for k in range(count):
        target = image_ref.at[pl.ds(k * SB, SB), :]
        pltpu.make_async_copy(mine_ref.at[pl.ds(0, SB), :], target, image_sems.at[k]).wait()
    load_dofs.wait()
    load_modes.wait()
    vectors = dot_f32(image_ref[...], factor_ref[...])
    own_ref[...] = vectors[: 2 * SB, :]
    touched = vectors[2 * SB :, :].astype(jnp.bfloat16)
    amplitude = lax.dot_general(
        touched,
        dofs_ref[...].reshape(KB * SB, dofs_ref.shape[2]),
        (((0,), (0,)), ((), ())),
        preferred_element_type=jnp.float32,
    )
    terms = (weight_ref[...] * amplitude).astype(jnp.bfloat16)
    stores = []
    for c in range(4):
        part = pl.ds(c * step, step)
        result_ref[part, :] = lax.dot_general(
            local_ref[part, :], terms, (((1,), (1,)), ((), ())), preferred_element_type=jnp.float32
        ).astype(jnp.bfloat16)
        stores.append(
            pltpu.make_async_copy(result_ref.at[part, :], interior_ref.at[part, :], result_sems.at[c])
        )
        stores[-1].start()
    for store in stores:
        store.wait()


def last_products(place, here, gram, gram_twin, mine, twin, weight, gathered, modes, scale):
    width = gram.shape[1]
    rows, count = modes.shape
    scalars = pl.BlockSpec(memory_space=pltpu.SMEM)
    anywhere = pl.BlockSpec(memory_space=pl.ANY)
    return pl.pallas_call(
        lambda *refs: last_kernel(scale, *refs),
        in_specs=[scalars, scalars, WHOLE, WHOLE, anywhere, anywhere, WHOLE, anywhere, anywhere],
        out_specs=(WHOLE, WHOLE, anywhere),
        out_shape=(
            jax.ShapeDtypeStruct((2 * SB, width), jnp.float32),
            jax.ShapeDtypeStruct((1, width), jnp.float32),
            jax.ShapeDtypeStruct((rows, width), jnp.bfloat16),
        ),
        scratch_shapes=[
            pltpu.VMEM((width, width), jnp.float32),
            pltpu.VMEM((width // 2, width // 2), jnp.float32),
            pltpu.VMEM((width // 2, width // 2), jnp.float32),
            pltpu.VMEM(((2 + KB) * SB, width), jnp.float32),
            pltpu.VMEM((gathered.shape[0], gathered.shape[1] // 2, count), jnp.bfloat16),
            pltpu.VMEM((rows, count), jnp.bfloat16),
            pltpu.VMEM((rows, width), jnp.bfloat16),
            pltpu.SemaphoreType.DMA((2 + KB,)),
            pltpu.SemaphoreType.DMA,
            pltpu.SemaphoreType.DMA,
            pltpu.SemaphoreType.DMA((4,)),
        ],
        compiler_params=pltpu.CompilerParams(vmem_limit_bytes=VMEM_BYTES),
        cost_estimate=pl.CostEstimate(
            flops=16_000_000_000, bytes_accessed=8_000_000, transcendentals=256
        ),
        name="last",
    )(place, here, gram, gram_twin, mine, twin, weight, gathered, modes)


def gather_blocks(x, axis):
    count = lax.axis_size(axis)
    spread = jnp.broadcast_to(x[None], (count,) + x.shape)
    return lax.all_to_all(spread, axis, 0, 0, tiled=True)


def per_device(modes, coupling, eigvals, mode_count, sep_map, sep_len, flex, init_vectors):
    shapes = modes[0]
    sep_count = lax.axis_size("sep")
    sub_count = lax.axis_size("sub")
    sep_index = lax.axis_index("sep")
    sub_index = lax.axis_index("sub")
    layers = sub_count // 2
    layer, core = sub_index >> 1, sub_index & 1
    mode_total = shapes.shape[1]
    vec_width = init_vectors.shape[1]
    owned_rows = init_vectors.shape[0]
    total_rows = owned_rows * sep_count
    local_dofs = KB * SB
    slim = SB // layers
    scaling = float(total_rows) ** 0.5

    def from_twin(x):
        return lax.ppermute(x, "sub", [(i, i ^ 1) for i in range(sub_count)])

    share = local_dofs // sep_count
    partial = lax.dot_general(
        coupling[0], shapes, (((0,), (0,)), ((), ())), preferred_element_type=jnp.float32
    )
    partial = partial.astype(jnp.bfloat16)
    shares = lax.all_to_all(
        partial.reshape(sep_count, share, mode_total), "sep", 0, 0, tiled=True
    )
    first_dof = sep_index * share
    length = lax.dynamic_index_in_dim(sep_len[0], first_dof // SB, 0, keepdims=False)
    live = first_dof % SB + jnp.arange(share, dtype=jnp.int32) < length
    own_projected = jnp.sum(shares.astype(jnp.float32), axis=0)
    own_projected = jnp.where(live[:, None], own_projected, 0.0).astype(jnp.bfloat16)
    fold = mode_total // vec_width
    start_rows = lax.dynamic_slice_in_dim(init_vectors, core * SB, SB, 0).astype(jnp.bfloat16)
    start_rows = jnp.concatenate([start_rows[share * q : share * (q + 1)] for q in range(fold)], axis=1)
    gathered = gather_blocks(jnp.concatenate([own_projected, start_rows], axis=0), "sep")
    mode_ids = jnp.arange(mode_total, dtype=jnp.int32)[None]
    mode_weight = jnp.where(mode_ids < mode_count[0], 1.0 / eigvals, 0.0)

    blocks = sep_map[0]
    outgoing, start_half = operator_rows(
        blocks, (2 * sep_index)[None], mode_weight, gathered, slim
    )
    start_half = start_half.reshape(total_rows // 2, vec_width)
    start_twin = from_twin(start_half)
    incoming = lax.all_to_all(outgoing, "sub", 0, 0, tiled=True)
    map_all = incoming[:, 0, local_dofs : local_dofs + KB].astype(jnp.int32).reshape(-1)

    row_start = core * SB + layer * slim
    flex_rows = lax.dynamic_slice_in_dim(flex, row_start, slim, 0)
    first_rows, own_half, twin_half = build_rows(
        map_all, core[None], incoming, flex_rows, start_half, start_twin
    )
    operator_half = jnp.concatenate([own_half, from_twin(twin_half)], axis=0)

    def from_layer(x, distance):
        perm = [(z * 2 + c, (z ^ distance) * 2 + c) for z in range(layers) for c in range(2)]
        return lax.ppermute(x, "sub", perm)

    def gather_half(rows, after):
        other = from_layer(rows, 4)
        upper = (layer & 4) > 0
        pair = jnp.stack([jnp.where(upper, other, rows), jnp.where(upper, rows, other)])
        pieces = [pair] + [from_layer(pair, distance) for distance in (1, 2, 3)]
        spread = spread_rows((layer & 3)[None], pieces, after, sep_count)
        whole = lax.all_to_all(spread, "sep", 0, 0, tiled=True)
        return whole.reshape(total_rows // 2, vec_width), spread

    first_half, _ = gather_half(first_rows, operator_half)
    both_rows = dot_f32(operator_half, first_half)
    second_rows = both_rows[:slim] + from_twin(both_rows[slim:])
    raw_half, second_spread = gather_half(second_rows, second_rows)

    first_gram = gram_of(first_half, second_spread)
    first_factor = inverse_transposed_factor(first_gram, from_twin(first_gram), scaling)
    iterate_half = iterate_of(first_half, first_factor)

    image_half, second_sums = image_and_sums(raw_half, iterate_half, first_factor)
    wanted = jnp.concatenate([2 * sep_index + jnp.arange(2, dtype=jnp.int32), blocks])
    separator_modes, quotient, interior = last_products(
        wanted >> 1,
        ((wanted & 1) == core).astype(jnp.int32),
        second_sums,
        from_twin(second_sums),
        image_half,
        from_twin(image_half),
        mode_weight,
        gathered,
        shapes,
        scaling,
    )
    return (separator_modes, quotient[0], interior[None])


def solution(mesh):
    placed = (
        P("sub", "sep", None),
        P("sub", "sep", None),
        P("sub", None),
        P("sub"),
        P("sub", None),
        P("sub", None),
        P("sep", None),
        P("sep", None),
    )
    return jax.shard_map(
        per_device,
        mesh=mesh,
        in_specs=placed,
        out_specs=(P("sep", None), P(), P("sub", "sep", None)),
        check_vma=False,
    )
```

```python
import jax
import jax.numpy as jnp
from jax import lax
from jax.experimental import pallas as pl
from jax.experimental.pallas import tpu as pltpu
from jax.sharding import PartitionSpec as P

KB = 4
SB = 128
CHUNK = 2048
VMEM_BYTES = 20 * 1024 * 1024
HIGHEST = lax.Precision.HIGHEST
WHOLE = pl.BlockSpec(memory_space=pltpu.VMEM)


def dot_f32(a, b, contract=((1,), (0,))):
    return lax.dot_general(
        a, b, (contract, ((), ())), precision=HIGHEST, preferred_element_type=jnp.float32
    )


def split_three(x):
    high = x.astype(jnp.bfloat16)
    rest = x - high.astype(jnp.float32)
    middle = rest.astype(jnp.bfloat16)
    return high, middle, (rest - middle.astype(jnp.float32)).astype(jnp.bfloat16)


def invert_factor(left_ref, right_ref):
    n = left_ref.shape[0]
    subs = lax.broadcasted_iota(jnp.int32, (8, n), 0)
    lanes = lax.broadcasted_iota(jnp.int32, (8, n), 1)

    def spread(x, row, lane):
        return jnp.broadcast_to(x[row : row + 1, lane : lane + 1], (8, n))

    def row_of(x, row):
        return jnp.broadcast_to(x[row : row + 1, :], (8, n))

    def stacked(pieces, base):
        out = base
        for row, piece in pieces:
            out = jnp.where(subs == row, piece, out)
        return out

    def panel(t, carry):
        start = pl.multiple_of(8 * t, 8)
        shift = (n - 8 * t) & (n - 1)
        pivots = left_ref[pl.ds(start, 8), :]
        pivots_right = right_ref[pl.ds(start, 8), :]
        corner = pltpu.roll(pivots, shift, 1)
        a = {(i, j): spread(corner, i, j) for i in range(8) for j in range(i + 1)}
        inverse, m = [], {}
        for j in range(8):
            inverse.append(1.0 / a[j, j])
            for i in range(j + 1, 8):
                m[i, j] = a[i, j] * inverse[j]
            for i in range(j + 1, 8):
                for k in range(j + 1, i + 1):
                    a[i, k] = a[i, k] - m[i, j] * a[k, j]
        unit = {}
        for i in range(8):
            for k in range(i):
                total = -m[i, k]
                for j in range(k + 1, i):
                    total = total - m[i, j] * unit[j, k]
                unit[i, k] = total
        zero = jnp.zeros((8, n), jnp.float32)
        down = [stacked([(i, unit[i, k]) for i in range(k + 1, 8)], zero) for k in range(7)]
        up = [stacked([(k, unit[i, k]) for k in range(i)], zero) for i in range(1, 8)]
        scale = stacked([(i, inverse[i]) for i in range(1, 8)], inverse[0])
        root = stacked([(i, a[i, i]) for i in range(1, 8)], a[0, 0])

        def reduce_rows(x):
            for_out = x
            for k in range(7):
                for_out = for_out + down[k] * row_of(x, k)
            scaled = for_out * scale
            back = scaled
            for i in range(1, 8):
                back = back + up[i - 1] * row_of(scaled, i)
            return for_out, back

        _, back_left = reduce_rows(pivots)
        done_right, back_right = reduce_rows(pivots_right)
        heads = jnp.where(lanes > 8 * t + 7, pivots, 0.0)
        upper = split_three(heads)
        lower = split_three(jnp.concatenate([back_left, back_right], axis=1))
        pairs = ((0, 0), (0, 1), (1, 0), (0, 2), (2, 0), (1, 1))
        change = lax.dot_general(
            jnp.concatenate([upper[p] for p, _ in pairs], axis=0),
            jnp.concatenate([lower[q] for _, q in pairs], axis=0),
            (((0,), (0,)), ((), ())),
            preferred_element_type=jnp.float32,
        )
        left_ref[...] = left_ref[...] - change[:, :n]
        right_ref[...] = right_ref[...] - change[:, n:]
        right_ref[pl.ds(start, 8), :] = done_right * lax.rsqrt(root)
        return carry

    lax.fori_loop(0, n // 8, panel, 0)


def factor_kernel(scale, gram_ref, twin_ref, out_ref, left_ref, right_ref):
    half = gram_ref.shape[1] // 2
    identity = jnp.where(
        lax.broadcasted_iota(jnp.int32, (half, half), 0)
        == lax.broadcasted_iota(jnp.int32, (half, half), 1),
        1.0,
        0.0,
    ).astype(jnp.float32)
    left_ref[...] = gram_ref[:half, :half] + twin_ref[:half, :half]
    right_ref[...] = identity
    invert_factor(left_ref, right_ref)
    first = right_ref[...]
    below = dot_f32(gram_ref[half : 2 * half, :half] + twin_ref[half : 2 * half, :half], first, ((1,), (1,)))
    left_ref[...] = (
        gram_ref[half : 2 * half, half:] + twin_ref[half : 2 * half, half:]
    ) - dot_f32(below, below, ((1,), (1,)))
    right_ref[...] = identity
    invert_factor(left_ref, right_ref)
    second = right_ref[...]
    corner = -dot_f32(second, dot_f32(below, first))
    out_ref[:half, :half] = first.T * scale
    out_ref[:half, half:] = corner.T * scale
    out_ref[half:, :half] = jnp.zeros((half, half), jnp.float32)
    out_ref[half:, half:] = second.T * scale


def inverse_transposed_factor(gram, twin, scale):
    half = gram.shape[0] // 2
    return pl.pallas_call(
        lambda *refs: factor_kernel(scale, *refs),
        out_shape=jax.ShapeDtypeStruct(gram.shape, jnp.float32),
        in_specs=[pl.BlockSpec(memory_space=pltpu.VMEM)] * 2,
        out_specs=pl.BlockSpec(memory_space=pltpu.VMEM),
        scratch_shapes=[pltpu.VMEM((half, half), jnp.float32)] * 2,
        compiler_params=pltpu.CompilerParams(vmem_limit_bytes=VMEM_BYTES),
        cost_estimate=pl.CostEstimate(
            flops=12_000_000_000, bytes_accessed=800_000, transcendentals=256
        ),
        name="factor",
    )(gram, twin)


def gram_step(x, even_ref, odd_ref):
    high, middle, low = split_three(x)

    def product(a, b):
        return lax.dot_general(
            a, b, (((0,), (0,)), ((), ())), preferred_element_type=jnp.float32
        )

    even_ref[...] += product(high, high) + product(middle, middle)
    odd_ref[...] += product(high, middle) + product(high, low)


def gram_kernel(x_ref, after_ref, out_ref, even_ref, odd_ref):
    even_ref[...] = jnp.zeros_like(even_ref)
    odd_ref[...] = jnp.zeros_like(odd_ref)

    def chunk(c, carry):
        gram_step(x_ref[pl.ds(pl.multiple_of(c * CHUNK, CHUNK), CHUNK), :], even_ref, odd_ref)
        return carry

    lax.fori_loop(0, x_ref.shape[0] // CHUNK, chunk, 0)
    out_ref[...] = even_ref[...] + odd_ref[...] + odd_ref[...].T


def gram_of(x, after):
    width = x.shape[1]
    return pl.pallas_call(
        gram_kernel,
        out_shape=jax.ShapeDtypeStruct((width, width), jnp.float32),
        in_specs=[WHOLE, pl.BlockSpec(memory_space=pl.ANY)],
        out_specs=WHOLE,
        scratch_shapes=[pltpu.VMEM((width, width), jnp.float32)] * 2,
        compiler_params=pltpu.CompilerParams(vmem_limit_bytes=VMEM_BYTES),
        cost_estimate=pl.CostEstimate(
            flops=2_000_000_000, bytes_accessed=2_400_000, transcendentals=0
        ),
        name="gram",
    )(x, after)


def iterate_kernel(first_ref, factor_ref, iterate_ref):
    iterate_ref[...] = dot_f32(first_ref[...], factor_ref[...])


def iterate_of(first, factor):
    return pl.pallas_call(
        iterate_kernel,
        out_shape=jax.ShapeDtypeStruct(first.shape, jnp.float32),
        in_specs=[WHOLE, WHOLE],
        out_specs=WHOLE,
        compiler_params=pltpu.CompilerParams(vmem_limit_bytes=VMEM_BYTES),
        cost_estimate=pl.CostEstimate(
            flops=2_000_000_000, bytes_accessed=4_000_000, transcendentals=0
        ),
        name="iterate",
    )(first, factor)


def image_kernel(
    place_ref, raw_ref, iterate_ref, factor_ref, image_ref, picks_ref, out_ref, even_ref, odd_ref
):
    width = even_ref.shape[0]
    even_ref[...] = jnp.zeros_like(even_ref)
    odd_ref[...] = jnp.zeros_like(odd_ref)
    image = dot_f32(raw_ref[...], factor_ref[...])
    image_ref[...] = image
    for k in range(1 + KB):
        source = pl.ds(pl.multiple_of(place_ref[k] * SB, SB), SB)
        picks_ref[k * SB : (k + 1) * SB, :] = image_ref[source, :]
    gram_step(image, even_ref, odd_ref)
    iterate = iterate_ref[...]
    out_ref[width:, :] = jnp.zeros((out_ref.shape[0] - width, width), jnp.float32)
    out_ref[width : width + 1, :] = jnp.sum(iterate * image, axis=0, keepdims=True)
    out_ref[width + 1 : width + 2, :] = jnp.sum(iterate * iterate, axis=0, keepdims=True)
    out_ref[:width, :] = even_ref[...] + odd_ref[...] + odd_ref[...].T


def image_and_sums(place, raw, iterate, factor):
    rows, width = raw.shape
    return pl.pallas_call(
        image_kernel,
        out_shape=(
            jax.ShapeDtypeStruct((rows, width), jnp.float32),
            jax.ShapeDtypeStruct(((1 + KB) * SB, width), jnp.float32),
            jax.ShapeDtypeStruct((width + 8, width), jnp.float32),
        ),
        in_specs=[pl.BlockSpec(memory_space=pltpu.SMEM), WHOLE, WHOLE, WHOLE],
        out_specs=(WHOLE, WHOLE, WHOLE),
        scratch_shapes=[pltpu.VMEM((width, width), jnp.float32)] * 2,
        compiler_params=pltpu.CompilerParams(vmem_limit_bytes=VMEM_BYTES),
        cost_estimate=pl.CostEstimate(
            flops=3_000_000_000, bytes_accessed=7_000_000, transcendentals=0
        ),
        name="image",
    )(place, raw, iterate, factor)


def spread_kernel(low_ref, own_ref, one_ref, two_ref, three_ref, after_ref, out_ref, part_ref, sems):
    slim = own_ref.shape[1]
    for e, piece_ref in enumerate((own_ref, one_ref, two_ref, three_ref)):
        for b in range(2):
            place = (4 * b + (low_ref[0] ^ e)) * slim
            part_ref[pl.ds(pl.multiple_of(place, slim), slim), :] = piece_ref[b]
    copies = [
        pltpu.make_async_copy(part_ref, out_ref.at[k], sems.at[k]) for k in range(out_ref.shape[0])
    ]
    for copy in copies:
        copy.start()
    for copy in copies:
        copy.wait()


def spread_rows(low, pieces, after, count):
    slim, width = pieces[0].shape[1:]
    anywhere = pl.BlockSpec(memory_space=pl.ANY)
    return pl.pallas_call(
        spread_kernel,
        out_shape=jax.ShapeDtypeStruct((count, 8 * slim, width), jnp.float32),
        in_specs=[pl.BlockSpec(memory_space=pltpu.SMEM)] + [WHOLE] * 4 + [anywhere],
        out_specs=anywhere,
        scratch_shapes=[
            pltpu.VMEM((8 * slim, width), jnp.float32),
            pltpu.SemaphoreType.DMA((count,)),
        ],
        cost_estimate=pl.CostEstimate(flops=0, bytes_accessed=2_400_000, transcendentals=0),
        name="spread",
    )(low, *pieces, after)


def rows_kernel(blocks_ref, first_ref, weight_ref, gathered_ref, out_ref, start_ref):
    slim = out_ref.shape[1]
    sources, height, modes = gathered_ref.shape
    height = height // 2
    dofs = sources * height
    width = start_ref.shape[2]
    for q in range(modes // width):
        start_ref[:, height * q : height * (q + 1), :] = gathered_ref[
            :, height:, width * q : width * (q + 1)
        ]
    everything = gathered_ref[:, :height, :].reshape(dofs, modes)
    lane = lax.broadcasted_iota(jnp.int32, (slim, SB), 1)
    numbers = jnp.zeros((slim, SB), jnp.int32)
    for k in range(KB):
        numbers = jnp.where(lane == k, blocks_ref[k], numbers)
    numbers = numbers.astype(jnp.float32).astype(jnp.bfloat16)
    for h in range(2):
        wanted = first_ref[0] + h
        place = jnp.int32(0)
        found = jnp.int32(0)
        for k in range(KB):
            hit = (blocks_ref[k] == wanted).astype(jnp.int32)
            place += k * hit
            found += hit
        span = sources // KB
        picked = gathered_ref[pl.ds(place * span, span), :height, :].reshape(SB, modes)
        weighted = picked.astype(jnp.float32) * (weight_ref[...] * found.astype(jnp.float32))
        high, middle, low = split_three(weighted)

        def product(part):
            return lax.dot_general(
                part, everything, (((1,), (1,)), ((), ())), preferred_element_type=jnp.float32
            )

        rows = (product(high) + (product(middle) + product(low))).astype(jnp.bfloat16)
        for z in range(SB // slim):
            out_ref[2 * z + h, :, :dofs] = rows[z * slim : (z + 1) * slim, :]
            out_ref[2 * z + h, :, dofs:] = numbers


def operator_rows(blocks, first, weight, gathered, slim):
    sources, height, modes = gathered.shape
    dofs = sources * height // 2
    width = height * modes // 2 // SB
    scalars = pl.BlockSpec(memory_space=pltpu.SMEM)
    return pl.pallas_call(
        rows_kernel,
        out_shape=(
            jax.ShapeDtypeStruct((2 * SB // slim, slim, dofs + SB), jnp.bfloat16),
            jax.ShapeDtypeStruct((sources, SB, width), jnp.bfloat16),
        ),
        in_specs=[scalars, scalars, WHOLE, WHOLE],
        out_specs=(WHOLE, WHOLE),
        compiler_params=pltpu.CompilerParams(vmem_limit_bytes=VMEM_BYTES),
        cost_estimate=pl.CostEstimate(
            flops=800_000_000, bytes_accessed=2_700_000, transcendentals=0
        ),
        name="rows",
    )(blocks, first, weight, gathered)


def build_kernel(
    map_ref, core_ref, incoming_ref, flex_ref, start_ref, twin_ref,
    rows_ref, own_ref, other_ref, halves_ref,
):
    slim, total = flex_ref.shape
    for b in range(total // SB):
        halves_ref[b % 2, :, (b // 2) * SB : (b // 2 + 1) * SB] = flex_ref[
            :, b * SB : (b + 1) * SB
        ]
    for s in range(incoming_ref.shape[0]):
        for k in range(KB):
            b = map_ref[s * KB + k]
            place = pl.ds(pl.multiple_of((b >> 1) * SB, SB), SB)
            halves_ref[b & 1, :, place] += incoming_ref[s, :, k * SB : (k + 1) * SB].astype(
                jnp.float32
            )
    own = halves_ref[core_ref[0]]
    other = halves_ref[1 - core_ref[0]]
    own_ref[...] = own
    other_ref[...] = other
    first = jnp.dot(
        jnp.concatenate(split_three(own), axis=0), start_ref[...], preferred_element_type=jnp.float32
    )
    second = jnp.dot(
        jnp.concatenate(split_three(other), axis=0), twin_ref[...], preferred_element_type=jnp.float32
    )
    both = first + second
    rows_ref[...] = both[:slim] + (both[slim : 2 * slim] + both[2 * slim :])


def build_rows(map_all, core, incoming, flex, start, twin):
    slim = incoming.shape[1]
    total = flex.shape[1]
    width = start.shape[1]
    scalars = pl.BlockSpec(memory_space=pltpu.SMEM)
    half = jax.ShapeDtypeStruct((slim, total // 2), jnp.float32)
    return pl.pallas_call(
        build_kernel,
        out_shape=(jax.ShapeDtypeStruct((slim, width), jnp.float32), half, half),
        in_specs=[scalars] * 2 + [WHOLE] * 4,
        out_specs=(WHOLE, WHOLE, WHOLE),
        scratch_shapes=[
            pltpu.VMEM((2, slim, total // 2), jnp.float32),
        ],
        compiler_params=pltpu.CompilerParams(vmem_limit_bytes=VMEM_BYTES),
        cost_estimate=pl.CostEstimate(
            flops=300_000_000, bytes_accessed=4_000_000, transcendentals=0
        ),
        name="build",
    )(map_all, core, incoming, flex, start, twin)


def last_kernel(
    scale,
    place_ref, here_ref, gram_ref, gram_twin_ref, mine_ref, twin_ref, weight_ref, gathered_ref,
    modes_ref, own_ref, quotient_ref, interior_ref, factor_ref, left_ref, right_ref, image_ref, dofs_ref,
    local_ref, result_ref, image_sems, mode_sem, dofs_sem, result_sems,
):
    count = 2 + KB
    rows = local_ref.shape[0]
    step = rows // 4
    load_modes = pltpu.make_async_copy(modes_ref, local_ref, mode_sem)
    load_dofs = pltpu.make_async_copy(
        gathered_ref.at[:, pl.ds(0, dofs_ref.shape[1]), :], dofs_ref, dofs_sem
    )
    for k in range(count):
        source = pl.ds(pl.multiple_of(place_ref[k] * SB, SB), SB)
        target = image_ref.at[pl.ds(k * SB, SB), :]

        @pl.when(here_ref[k] == 1)
        def _():
            pltpu.make_async_copy(mine_ref.at[source, :], target, image_sems.at[k]).start()

        @pl.when(here_ref[k] != 1)
        def _():
            picked = pl.ds((0 if k < 2 else k - 1) * SB, SB)
            pltpu.make_async_copy(twin_ref.at[picked, :], target, image_sems.at[k]).start()

    load_modes.start()
    load_dofs.start()
    width = gram_ref.shape[1]
    sums = gram_ref[width:, :] + gram_twin_ref[width:, :]
    quotient_ref[...] = sums[0:1, :] / sums[1:2, :]
    factor_kernel(scale, gram_ref, gram_twin_ref, factor_ref, left_ref, right_ref)
    for k in range(count):
        target = image_ref.at[pl.ds(k * SB, SB), :]
        pltpu.make_async_copy(mine_ref.at[pl.ds(0, SB), :], target, image_sems.at[k]).wait()
    load_dofs.wait()
    load_modes.wait()
    vectors = dot_f32(image_ref[...], factor_ref[...])
    own_ref[...] = vectors[: 2 * SB, :]
    touched = vectors[2 * SB :, :].astype(jnp.bfloat16)
    amplitude = lax.dot_general(
        touched,
        dofs_ref[...].reshape(KB * SB, dofs_ref.shape[2]),
        (((0,), (0,)), ((), ())),
        preferred_element_type=jnp.float32,
    )
    terms = (weight_ref[...] * amplitude).astype(jnp.bfloat16)
    stores = []
    for c in range(4):
        part = pl.ds(c * step, step)
        result_ref[part, :] = lax.dot_general(
            local_ref[part, :], terms, (((1,), (1,)), ((), ())), preferred_element_type=jnp.float32
        ).astype(jnp.bfloat16)
        stores.append(
            pltpu.make_async_copy(result_ref.at[part, :], interior_ref.at[part, :], result_sems.at[c])
        )
        stores[-1].start()
    for store in stores:
        store.wait()


def last_products(place, here, gram, gram_twin, mine, twin, weight, gathered, modes, scale):
    width = gram.shape[1]
    rows, count = modes.shape
    scalars = pl.BlockSpec(memory_space=pltpu.SMEM)
    anywhere = pl.BlockSpec(memory_space=pl.ANY)
    return pl.pallas_call(
        lambda *refs: last_kernel(scale, *refs),
        in_specs=[scalars, scalars, WHOLE, WHOLE, anywhere, anywhere, WHOLE, anywhere, anywhere],
        out_specs=(WHOLE, WHOLE, anywhere),
        out_shape=(
            jax.ShapeDtypeStruct((2 * SB, width), jnp.float32),
            jax.ShapeDtypeStruct((1, width), jnp.float32),
            jax.ShapeDtypeStruct((rows, width), jnp.bfloat16),
        ),
        scratch_shapes=[
            pltpu.VMEM((width, width), jnp.float32),
            pltpu.VMEM((width // 2, width // 2), jnp.float32),
            pltpu.VMEM((width // 2, width // 2), jnp.float32),
            pltpu.VMEM(((2 + KB) * SB, width), jnp.float32),
            pltpu.VMEM((gathered.shape[0], gathered.shape[1] // 2, count), jnp.bfloat16),
            pltpu.VMEM((rows, count), jnp.bfloat16),
            pltpu.VMEM((rows, width), jnp.bfloat16),
            pltpu.SemaphoreType.DMA((2 + KB,)),
            pltpu.SemaphoreType.DMA,
            pltpu.SemaphoreType.DMA,
            pltpu.SemaphoreType.DMA((4,)),
        ],
        compiler_params=pltpu.CompilerParams(vmem_limit_bytes=VMEM_BYTES),
        cost_estimate=pl.CostEstimate(
            flops=16_000_000_000, bytes_accessed=8_000_000, transcendentals=256
        ),
        name="last",
    )(place, here, gram, gram_twin, mine, twin, weight, gathered, modes)


def gather_blocks(x, axis):
    count = lax.axis_size(axis)
    spread = jnp.broadcast_to(x[None], (count,) + x.shape)
    return lax.all_to_all(spread, axis, 0, 0, tiled=True)


def per_device(modes, coupling, eigvals, mode_count, sep_map, sep_len, flex, init_vectors):
    shapes = modes[0]
    sep_count = lax.axis_size("sep")
    sub_count = lax.axis_size("sub")
    sep_index = lax.axis_index("sep")
    sub_index = lax.axis_index("sub")
    layers = sub_count // 2
    layer, core = sub_index >> 1, sub_index & 1
    mode_total = shapes.shape[1]
    vec_width = init_vectors.shape[1]
    owned_rows = init_vectors.shape[0]
    total_rows = owned_rows * sep_count
    local_dofs = KB * SB
    slim = SB // layers
    scaling = float(total_rows) ** 0.5

    def from_twin(x):
        return lax.ppermute(x, "sub", [(i, i ^ 1) for i in range(sub_count)])

    share = local_dofs // sep_count
    partial = lax.dot_general(
        coupling[0], shapes, (((0,), (0,)), ((), ())), preferred_element_type=jnp.float32
    )
    partial = partial.astype(jnp.bfloat16)
    shares = lax.all_to_all(
        partial.reshape(sep_count, share, mode_total), "sep", 0, 0, tiled=True
    )
    first_dof = sep_index * share
    length = lax.dynamic_index_in_dim(sep_len[0], first_dof // SB, 0, keepdims=False)
    live = first_dof % SB + jnp.arange(share, dtype=jnp.int32) < length
    own_projected = jnp.sum(shares.astype(jnp.float32), axis=0)
    own_projected = jnp.where(live[:, None], own_projected, 0.0).astype(jnp.bfloat16)
    fold = mode_total // vec_width
    start_rows = lax.dynamic_slice_in_dim(init_vectors, core * SB, SB, 0).astype(jnp.bfloat16)
    start_rows = jnp.concatenate([start_rows[share * q : share * (q + 1)] for q in range(fold)], axis=1)
    gathered = gather_blocks(jnp.concatenate([own_projected, start_rows], axis=0), "sep")
    mode_ids = jnp.arange(mode_total, dtype=jnp.int32)[None]
    mode_weight = jnp.where(mode_ids < mode_count[0], 1.0 / eigvals, 0.0)

    blocks = sep_map[0]
    outgoing, start_half = operator_rows(
        blocks, (2 * sep_index)[None], mode_weight, gathered, slim
    )
    start_half = start_half.reshape(total_rows // 2, vec_width)
    start_twin = from_twin(start_half)
    incoming = lax.all_to_all(outgoing, "sub", 0, 0, tiled=True)
    map_all = incoming[:, 0, local_dofs : local_dofs + KB].astype(jnp.int32).reshape(-1)

    row_start = core * SB + layer * slim
    flex_rows = lax.dynamic_slice_in_dim(flex, row_start, slim, 0)
    first_rows, own_half, twin_half = build_rows(
        map_all, core[None], incoming, flex_rows, start_half, start_twin
    )
    operator_half = jnp.concatenate([own_half, from_twin(twin_half)], axis=0)

    def from_layer(x, distance):
        perm = [(z * 2 + c, (z ^ distance) * 2 + c) for z in range(layers) for c in range(2)]
        return lax.ppermute(x, "sub", perm)

    def gather_half(rows, after):
        other = from_layer(rows, 4)
        upper = (layer & 4) > 0
        pair = jnp.stack([jnp.where(upper, other, rows), jnp.where(upper, rows, other)])
        pieces = [pair] + [from_layer(pair, distance) for distance in (1, 2, 3)]
        spread = spread_rows((layer & 3)[None], pieces, after, sep_count)
        whole = lax.all_to_all(spread, "sep", 0, 0, tiled=True)
        return whole.reshape(total_rows // 2, vec_width), spread

    first_half, _ = gather_half(first_rows, operator_half)
    both_rows = dot_f32(operator_half, first_half)
    second_rows = both_rows[:slim] + from_twin(both_rows[slim:])
    raw_half, second_spread = gather_half(second_rows, second_rows)

    first_gram = gram_of(first_half, second_spread)
    first_factor = inverse_transposed_factor(first_gram, from_twin(first_gram), scaling)
    iterate_half = iterate_of(first_half, first_factor)

    twin_blocks = lax.dynamic_slice_in_dim(map_all, (sub_index ^ 1) * KB, KB, 0)
    image_half, picks, second_sums = image_and_sums(
        jnp.concatenate([sep_index[None], twin_blocks >> 1]), raw_half, iterate_half, first_factor
    )
    wanted = jnp.concatenate([2 * sep_index + jnp.arange(2, dtype=jnp.int32), blocks])
    separator_modes, quotient, interior = last_products(
        wanted >> 1,
        ((wanted & 1) == core).astype(jnp.int32),
        second_sums,
        from_twin(second_sums),
        image_half,
        from_twin(picks),
        mode_weight,
        gathered,
        shapes,
        scaling,
    )
    return (separator_modes, quotient[0], interior[None])


def solution(mesh):
    placed = (
        P("sub", "sep", None),
        P("sub", "sep", None),
        P("sub", None),
        P("sub"),
        P("sub", None),
        P("sub", None),
        P("sep", None),
        P("sep", None),
    )
    return jax.shard_map(
        per_device,
        mesh=mesh,
        in_specs=placed,
        out_specs=(P("sep", None), P(), P("sub", "sep", None)),
        check_vma=False,
    )
```

```python
import jax
import jax.numpy as jnp
from jax import lax
from jax.experimental import pallas as pl
from jax.experimental.pallas import tpu as pltpu
from jax.sharding import PartitionSpec as P

KB = 4
SB = 128
CHUNK = 2048
VMEM_BYTES = 20 * 1024 * 1024
HIGHEST = lax.Precision.HIGHEST
WHOLE = pl.BlockSpec(memory_space=pltpu.VMEM)


def dot_f32(a, b, contract=((1,), (0,))):
    return lax.dot_general(
        a, b, (contract, ((), ())), precision=HIGHEST, preferred_element_type=jnp.float32
    )


def split_three(x):
    high = x.astype(jnp.bfloat16)
    rest = x - high.astype(jnp.float32)
    middle = rest.astype(jnp.bfloat16)
    return high, middle, (rest - middle.astype(jnp.float32)).astype(jnp.bfloat16)


def invert_factor(left_ref, right_ref):
    n = left_ref.shape[0]
    subs = lax.broadcasted_iota(jnp.int32, (8, n), 0)
    lanes = lax.broadcasted_iota(jnp.int32, (8, n), 1)

    def spread(x, row, lane):
        return jnp.broadcast_to(x[row : row + 1, lane : lane + 1], (8, n))

    def row_of(x, row):
        return jnp.broadcast_to(x[row : row + 1, :], (8, n))

    def stacked(pieces, base):
        out = base
        for row, piece in pieces:
            out = jnp.where(subs == row, piece, out)
        return out

    def panel(t, carry):
        start = pl.multiple_of(8 * t, 8)
        shift = (n - 8 * t) & (n - 1)
        pivots = left_ref[pl.ds(start, 8), :]
        pivots_right = right_ref[pl.ds(start, 8), :]
        corner = pltpu.roll(pivots, shift, 1)
        a = {(i, j): spread(corner, i, j) for i in range(8) for j in range(i + 1)}
        inverse, m = [], {}
        for j in range(8):
            inverse.append(1.0 / a[j, j])
            for i in range(j + 1, 8):
                m[i, j] = a[i, j] * inverse[j]
            for i in range(j + 1, 8):
                for k in range(j + 1, i + 1):
                    a[i, k] = a[i, k] - m[i, j] * a[k, j]
        unit = {}
        for i in range(8):
            for k in range(i):
                total = -m[i, k]
                for j in range(k + 1, i):
                    total = total - m[i, j] * unit[j, k]
                unit[i, k] = total
        zero = jnp.zeros((8, n), jnp.float32)
        down = [stacked([(i, unit[i, k]) for i in range(k + 1, 8)], zero) for k in range(7)]
        up = [stacked([(k, unit[i, k]) for k in range(i)], zero) for i in range(1, 8)]
        scale = stacked([(i, inverse[i]) for i in range(1, 8)], inverse[0])
        root = stacked([(i, a[i, i]) for i in range(1, 8)], a[0, 0])

        def reduce_rows(x):
            for_out = x
            for k in range(7):
                for_out = for_out + down[k] * row_of(x, k)
            scaled = for_out * scale
            back = scaled
            for i in range(1, 8):
                back = back + up[i - 1] * row_of(scaled, i)
            return for_out, back

        _, back_left = reduce_rows(pivots)
        done_right, back_right = reduce_rows(pivots_right)
        heads = jnp.where(lanes > 8 * t + 7, pivots, 0.0)
        upper = split_three(heads)
        lower = split_three(jnp.concatenate([back_left, back_right], axis=1))
        pairs = ((0, 0), (0, 1), (1, 0), (0, 2), (2, 0), (1, 1))
        change = lax.dot_general(
            jnp.concatenate([upper[p] for p, _ in pairs], axis=0),
            jnp.concatenate([lower[q] for _, q in pairs], axis=0),
            (((0,), (0,)), ((), ())),
            preferred_element_type=jnp.float32,
        )
        left_ref[...] = left_ref[...] - change[:, :n]
        right_ref[...] = right_ref[...] - change[:, n:]
        right_ref[pl.ds(start, 8), :] = done_right * lax.rsqrt(root)
        return carry

    lax.fori_loop(0, n // 8, panel, 0)


def factor_kernel(scale, gram_ref, twin_ref, out_ref, left_ref, right_ref):
    half = gram_ref.shape[1] // 2
    identity = jnp.where(
        lax.broadcasted_iota(jnp.int32, (half, half), 0)
        == lax.broadcasted_iota(jnp.int32, (half, half), 1),
        1.0,
        0.0,
    ).astype(jnp.float32)
    left_ref[...] = gram_ref[:half, :half] + twin_ref[:half, :half]
    right_ref[...] = identity
    invert_factor(left_ref, right_ref)
    first = right_ref[...]
    below = dot_f32(gram_ref[half : 2 * half, :half] + twin_ref[half : 2 * half, :half], first, ((1,), (1,)))
    left_ref[...] = (
        gram_ref[half : 2 * half, half:] + twin_ref[half : 2 * half, half:]
    ) - dot_f32(below, below, ((1,), (1,)))
    right_ref[...] = identity
    invert_factor(left_ref, right_ref)
    second = right_ref[...]
    corner = -dot_f32(second, dot_f32(below, first))
    out_ref[:half, :half] = first.T * scale
    out_ref[:half, half:] = corner.T * scale
    out_ref[half:, :half] = jnp.zeros((half, half), jnp.float32)
    out_ref[half:, half:] = second.T * scale


def inverse_transposed_factor(gram, twin, scale):
    half = gram.shape[0] // 2
    return pl.pallas_call(
        lambda *refs: factor_kernel(scale, *refs),
        out_shape=jax.ShapeDtypeStruct(gram.shape, jnp.float32),
        in_specs=[pl.BlockSpec(memory_space=pltpu.VMEM)] * 2,
        out_specs=pl.BlockSpec(memory_space=pltpu.VMEM),
        scratch_shapes=[pltpu.VMEM((half, half), jnp.float32)] * 2,
        compiler_params=pltpu.CompilerParams(vmem_limit_bytes=VMEM_BYTES),
        cost_estimate=pl.CostEstimate(
            flops=12_000_000_000, bytes_accessed=800_000, transcendentals=256
        ),
        name="factor",
    )(gram, twin)


def gram_step(x, even_ref, odd_ref):
    high, middle, low = split_three(x)

    def product(a, b):
        return lax.dot_general(
            a, b, (((0,), (0,)), ((), ())), preferred_element_type=jnp.float32
        )

    even_ref[...] += product(high, high) + product(middle, middle)
    odd_ref[...] += product(high, middle) + product(high, low)


def gram_kernel(x_ref, after_ref, out_ref, even_ref, odd_ref):
    even_ref[...] = jnp.zeros_like(even_ref)
    odd_ref[...] = jnp.zeros_like(odd_ref)

    def chunk(c, carry):
        gram_step(x_ref[pl.ds(pl.multiple_of(c * CHUNK, CHUNK), CHUNK), :], even_ref, odd_ref)
        return carry

    lax.fori_loop(0, x_ref.shape[0] // CHUNK, chunk, 0)
    out_ref[...] = even_ref[...] + odd_ref[...] + odd_ref[...].T


def gram_of(x, after):
    width = x.shape[1]
    return pl.pallas_call(
        gram_kernel,
        out_shape=jax.ShapeDtypeStruct((width, width), jnp.float32),
        in_specs=[WHOLE, pl.BlockSpec(memory_space=pl.ANY)],
        out_specs=WHOLE,
        scratch_shapes=[pltpu.VMEM((width, width), jnp.float32)] * 2,
        compiler_params=pltpu.CompilerParams(vmem_limit_bytes=VMEM_BYTES),
        cost_estimate=pl.CostEstimate(
            flops=2_000_000_000, bytes_accessed=2_400_000, transcendentals=0
        ),
        name="gram",
    )(x, after)


def iterate_kernel(first_ref, factor_ref, iterate_ref):
    iterate_ref[...] = dot_f32(first_ref[...], factor_ref[...])


def iterate_of(first, factor):
    return pl.pallas_call(
        iterate_kernel,
        out_shape=jax.ShapeDtypeStruct(first.shape, jnp.float32),
        in_specs=[WHOLE, WHOLE],
        out_specs=WHOLE,
        compiler_params=pltpu.CompilerParams(vmem_limit_bytes=VMEM_BYTES),
        cost_estimate=pl.CostEstimate(
            flops=2_000_000_000, bytes_accessed=4_000_000, transcendentals=0
        ),
        name="iterate",
    )(first, factor)


def image_kernel(
    place_ref, raw_ref, iterate_ref, factor_ref, image_ref, picks_ref, out_ref, even_ref, odd_ref
):
    width = even_ref.shape[0]
    even_ref[...] = jnp.zeros_like(even_ref)
    odd_ref[...] = jnp.zeros_like(odd_ref)
    image = dot_f32(raw_ref[...], factor_ref[...])
    image_ref[...] = image
    for k in range(1 + KB):
        source = pl.ds(pl.multiple_of(place_ref[k] * SB, SB), SB)
        picks_ref[k * SB : (k + 1) * SB, :] = image_ref[source, :]
    gram_step(image, even_ref, odd_ref)
    iterate = iterate_ref[...]
    out_ref[width:, :] = jnp.zeros((out_ref.shape[0] - width, width), jnp.float32)
    out_ref[width : width + 1, :] = jnp.sum(iterate * image, axis=0, keepdims=True)
    out_ref[width + 1 : width + 2, :] = jnp.sum(iterate * iterate, axis=0, keepdims=True)
    out_ref[:width, :] = even_ref[...] + odd_ref[...] + odd_ref[...].T


def image_and_sums(place, raw, iterate, factor):
    rows, width = raw.shape
    return pl.pallas_call(
        image_kernel,
        out_shape=(
            jax.ShapeDtypeStruct((rows, width), jnp.float32),
            jax.ShapeDtypeStruct(((1 + KB) * SB, width), jnp.float32),
            jax.ShapeDtypeStruct((width + 8, width), jnp.float32),
        ),
        in_specs=[pl.BlockSpec(memory_space=pltpu.SMEM), WHOLE, WHOLE, WHOLE],
        out_specs=(WHOLE, WHOLE, WHOLE),
        scratch_shapes=[pltpu.VMEM((width, width), jnp.float32)] * 2,
        compiler_params=pltpu.CompilerParams(vmem_limit_bytes=VMEM_BYTES),
        cost_estimate=pl.CostEstimate(
            flops=3_000_000_000, bytes_accessed=7_000_000, transcendentals=0
        ),
        name="image",
    )(place, raw, iterate, factor)


def spread_kernel(low_ref, own_ref, one_ref, two_ref, three_ref, after_ref, out_ref, part_ref, sems):
    slim = own_ref.shape[1]
    for e, piece_ref in enumerate((own_ref, one_ref, two_ref, three_ref)):
        for b in range(2):
            place = (4 * b + (low_ref[0] ^ e)) * slim
            part_ref[pl.ds(pl.multiple_of(place, slim), slim), :] = piece_ref[b]
    copies = [
        pltpu.make_async_copy(part_ref, out_ref.at[k], sems.at[k]) for k in range(out_ref.shape[0])
    ]
    for copy in copies:
        copy.start()
    for copy in copies:
        copy.wait()


def spread_rows(low, pieces, after, count):
    slim, width = pieces[0].shape[1:]
    anywhere = pl.BlockSpec(memory_space=pl.ANY)
    return pl.pallas_call(
        spread_kernel,
        out_shape=jax.ShapeDtypeStruct((count, 8 * slim, width), jnp.float32),
        in_specs=[pl.BlockSpec(memory_space=pltpu.SMEM)] + [WHOLE] * 4 + [anywhere],
        out_specs=anywhere,
        scratch_shapes=[
            pltpu.VMEM((8 * slim, width), jnp.float32),
            pltpu.SemaphoreType.DMA((count,)),
        ],
        compiler_params=pltpu.CompilerParams(vmem_limit_bytes=4 * 1024 * 1024),
        cost_estimate=pl.CostEstimate(flops=0, bytes_accessed=2_400_000, transcendentals=0),
        name="spread",
    )(low, *pieces, after)


def rows_kernel(blocks_ref, first_ref, weight_ref, gathered_ref, out_ref, start_ref):
    slim = out_ref.shape[1]
    sources, height, modes = gathered_ref.shape
    height = height // 2
    dofs = sources * height
    width = start_ref.shape[2]
    for q in range(modes // width):
        start_ref[:, height * q : height * (q + 1), :] = gathered_ref[
            :, height:, width * q : width * (q + 1)
        ]
    everything = gathered_ref[:, :height, :].reshape(dofs, modes)
    lane = lax.broadcasted_iota(jnp.int32, (slim, SB), 1)
    numbers = jnp.zeros((slim, SB), jnp.int32)
    for k in range(KB):
        numbers = jnp.where(lane == k, blocks_ref[k], numbers)
    numbers = numbers.astype(jnp.float32).astype(jnp.bfloat16)
    for h in range(2):
        wanted = first_ref[0] + h
        place = jnp.int32(0)
        found = jnp.int32(0)
        for k in range(KB):
            hit = (blocks_ref[k] == wanted).astype(jnp.int32)
            place += k * hit
            found += hit
        span = sources // KB
        picked = gathered_ref[pl.ds(place * span, span), :height, :].reshape(SB, modes)
        weighted = picked.astype(jnp.float32) * (weight_ref[...] * found.astype(jnp.float32))
        high, middle, low = split_three(weighted)

        def product(part):
            return lax.dot_general(
                part, everything, (((1,), (1,)), ((), ())), preferred_element_type=jnp.float32
            )

        rows = (product(high) + (product(middle) + product(low))).astype(jnp.bfloat16)
        for z in range(SB // slim):
            out_ref[2 * z + h, :, :dofs] = rows[z * slim : (z + 1) * slim, :]
            out_ref[2 * z + h, :, dofs:] = numbers


def operator_rows(blocks, first, weight, gathered, slim):
    sources, height, modes = gathered.shape
    dofs = sources * height // 2
    width = height * modes // 2 // SB
    scalars = pl.BlockSpec(memory_space=pltpu.SMEM)
    return pl.pallas_call(
        rows_kernel,
        out_shape=(
            jax.ShapeDtypeStruct((2 * SB // slim, slim, dofs + SB), jnp.bfloat16),
            jax.ShapeDtypeStruct((sources, SB, width), jnp.bfloat16),
        ),
        in_specs=[scalars, scalars, WHOLE, WHOLE],
        out_specs=(WHOLE, WHOLE),
        compiler_params=pltpu.CompilerParams(vmem_limit_bytes=VMEM_BYTES),
        cost_estimate=pl.CostEstimate(
            flops=800_000_000, bytes_accessed=2_700_000, transcendentals=0
        ),
        name="rows",
    )(blocks, first, weight, gathered)


def build_kernel(
    map_ref, core_ref, incoming_ref, flex_ref, start_ref, twin_ref,
    rows_ref, own_ref, other_ref, halves_ref,
):
    slim, total = flex_ref.shape
    for b in range(total // SB):
        halves_ref[b % 2, :, (b // 2) * SB : (b // 2 + 1) * SB] = flex_ref[
            :, b * SB : (b + 1) * SB
        ]
    for s in range(incoming_ref.shape[0]):
        for k in range(KB):
            b = map_ref[s * KB + k]
            place = pl.ds(pl.multiple_of((b >> 1) * SB, SB), SB)
            halves_ref[b & 1, :, place] += incoming_ref[s, :, k * SB : (k + 1) * SB].astype(
                jnp.float32
            )
    own = halves_ref[core_ref[0]]
    other = halves_ref[1 - core_ref[0]]
    own_ref[...] = own
    other_ref[...] = other
    first = jnp.dot(
        jnp.concatenate(split_three(own), axis=0), start_ref[...], preferred_element_type=jnp.float32
    )
    second = jnp.dot(
        jnp.concatenate(split_three(other), axis=0), twin_ref[...], preferred_element_type=jnp.float32
    )
    both = first + second
    rows_ref[...] = both[:slim] + (both[slim : 2 * slim] + both[2 * slim :])


def build_rows(map_all, core, incoming, flex, start, twin):
    slim = incoming.shape[1]
    total = flex.shape[1]
    width = start.shape[1]
    scalars = pl.BlockSpec(memory_space=pltpu.SMEM)
    half = jax.ShapeDtypeStruct((slim, total // 2), jnp.float32)
    return pl.pallas_call(
        build_kernel,
        out_shape=(jax.ShapeDtypeStruct((slim, width), jnp.float32), half, half),
        in_specs=[scalars] * 2 + [WHOLE] * 4,
        out_specs=(WHOLE, WHOLE, WHOLE),
        scratch_shapes=[
            pltpu.VMEM((2, slim, total // 2), jnp.float32),
        ],
        compiler_params=pltpu.CompilerParams(vmem_limit_bytes=VMEM_BYTES),
        cost_estimate=pl.CostEstimate(
            flops=300_000_000, bytes_accessed=4_000_000, transcendentals=0
        ),
        name="build",
    )(map_all, core, incoming, flex, start, twin)


def last_kernel(
    scale,
    place_ref, here_ref, gram_ref, gram_twin_ref, mine_ref, twin_ref, weight_ref, gathered_ref,
    modes_ref, own_ref, quotient_ref, interior_ref, factor_ref, left_ref, right_ref, image_ref, dofs_ref,
    local_ref, result_ref, image_sems, mode_sem, dofs_sem, result_sems,
):
    count = 2 + KB
    rows = local_ref.shape[0]
    step = rows // 4
    load_modes = pltpu.make_async_copy(modes_ref, local_ref, mode_sem)
    load_dofs = pltpu.make_async_copy(
        gathered_ref.at[:, pl.ds(0, dofs_ref.shape[1]), :], dofs_ref, dofs_sem
    )
    for k in range(count):
        source = pl.ds(pl.multiple_of(place_ref[k] * SB, SB), SB)
        target = image_ref.at[pl.ds(k * SB, SB), :]

        @pl.when(here_ref[k] == 1)
        def _():
            pltpu.make_async_copy(mine_ref.at[source, :], target, image_sems.at[k]).start()

        @pl.when(here_ref[k] != 1)
        def _():
            picked = pl.ds((0 if k < 2 else k - 1) * SB, SB)
            pltpu.make_async_copy(twin_ref.at[picked, :], target, image_sems.at[k]).start()

    load_modes.start()
    load_dofs.start()
    width = gram_ref.shape[1]
    sums = gram_ref[width:, :] + gram_twin_ref[width:, :]
    quotient_ref[...] = sums[0:1, :] / sums[1:2, :]
    factor_kernel(scale, gram_ref, gram_twin_ref, factor_ref, left_ref, right_ref)
    for k in range(count):
        target = image_ref.at[pl.ds(k * SB, SB), :]
        pltpu.make_async_copy(mine_ref.at[pl.ds(0, SB), :], target, image_sems.at[k]).wait()
    load_dofs.wait()
    load_modes.wait()
    vectors = dot_f32(image_ref[...], factor_ref[...])
    own_ref[...] = vectors[: 2 * SB, :]
    touched = vectors[2 * SB :, :].astype(jnp.bfloat16)
    amplitude = lax.dot_general(
        touched,
        dofs_ref[...].reshape(KB * SB, dofs_ref.shape[2]),
        (((0,), (0,)), ((), ())),
        preferred_element_type=jnp.float32,
    )
    terms = (weight_ref[...] * amplitude).astype(jnp.bfloat16)
    stores = []
    for c in range(4):
        part = pl.ds(c * step, step)
        result_ref[part, :] = lax.dot_general(
            local_ref[part, :], terms, (((1,), (1,)), ((), ())), preferred_element_type=jnp.float32
        ).astype(jnp.bfloat16)
        stores.append(
            pltpu.make_async_copy(result_ref.at[part, :], interior_ref.at[part, :], result_sems.at[c])
        )
        stores[-1].start()
    for store in stores:
        store.wait()


def last_products(place, here, gram, gram_twin, mine, twin, weight, gathered, modes, scale):
    width = gram.shape[1]
    rows, count = modes.shape
    scalars = pl.BlockSpec(memory_space=pltpu.SMEM)
    anywhere = pl.BlockSpec(memory_space=pl.ANY)
    return pl.pallas_call(
        lambda *refs: last_kernel(scale, *refs),
        in_specs=[scalars, scalars, WHOLE, WHOLE, anywhere, anywhere, WHOLE, anywhere, anywhere],
        out_specs=(WHOLE, WHOLE, anywhere),
        out_shape=(
            jax.ShapeDtypeStruct((2 * SB, width), jnp.float32),
            jax.ShapeDtypeStruct((1, width), jnp.float32),
            jax.ShapeDtypeStruct((rows, width), jnp.bfloat16),
        ),
        scratch_shapes=[
            pltpu.VMEM((width, width), jnp.float32),
            pltpu.VMEM((width // 2, width // 2), jnp.float32),
            pltpu.VMEM((width // 2, width // 2), jnp.float32),
            pltpu.VMEM(((2 + KB) * SB, width), jnp.float32),
            pltpu.VMEM((gathered.shape[0], gathered.shape[1] // 2, count), jnp.bfloat16),
            pltpu.VMEM((rows, count), jnp.bfloat16),
            pltpu.VMEM((rows, width), jnp.bfloat16),
            pltpu.SemaphoreType.DMA((2 + KB,)),
            pltpu.SemaphoreType.DMA,
            pltpu.SemaphoreType.DMA,
            pltpu.SemaphoreType.DMA((4,)),
        ],
        compiler_params=pltpu.CompilerParams(vmem_limit_bytes=VMEM_BYTES),
        cost_estimate=pl.CostEstimate(
            flops=16_000_000_000, bytes_accessed=8_000_000, transcendentals=256
        ),
        name="last",
    )(place, here, gram, gram_twin, mine, twin, weight, gathered, modes)


def gather_blocks(x, axis):
    count = lax.axis_size(axis)
    spread = jnp.broadcast_to(x[None], (count,) + x.shape)
    return lax.all_to_all(spread, axis, 0, 0, tiled=True)


def per_device(modes, coupling, eigvals, mode_count, sep_map, sep_len, flex, init_vectors):
    shapes = modes[0]
    sep_count = lax.axis_size("sep")
    sub_count = lax.axis_size("sub")
    sep_index = lax.axis_index("sep")
    sub_index = lax.axis_index("sub")
    layers = sub_count // 2
    layer, core = sub_index >> 1, sub_index & 1
    mode_total = shapes.shape[1]
    vec_width = init_vectors.shape[1]
    owned_rows = init_vectors.shape[0]
    total_rows = owned_rows * sep_count
    local_dofs = KB * SB
    slim = SB // layers
    scaling = float(total_rows) ** 0.5

    def from_twin(x):
        return lax.ppermute(x, "sub", [(i, i ^ 1) for i in range(sub_count)])

    share = local_dofs // sep_count
    partial = lax.dot_general(
        coupling[0], shapes, (((0,), (0,)), ((), ())), preferred_element_type=jnp.float32
    )
    partial = partial.astype(jnp.bfloat16)
    shares = lax.all_to_all(
        partial.reshape(sep_count, share, mode_total), "sep", 0, 0, tiled=True
    )
    first_dof = sep_index * share
    length = lax.dynamic_index_in_dim(sep_len[0], first_dof // SB, 0, keepdims=False)
    live = first_dof % SB + jnp.arange(share, dtype=jnp.int32) < length
    own_projected = jnp.sum(shares.astype(jnp.float32), axis=0)
    own_projected = jnp.where(live[:, None], own_projected, 0.0).astype(jnp.bfloat16)
    fold = mode_total // vec_width
    start_rows = lax.dynamic_slice_in_dim(init_vectors, core * SB, SB, 0).astype(jnp.bfloat16)
    start_rows = jnp.concatenate([start_rows[share * q : share * (q + 1)] for q in range(fold)], axis=1)
    gathered = gather_blocks(jnp.concatenate([own_projected, start_rows], axis=0), "sep")
    mode_ids = jnp.arange(mode_total, dtype=jnp.int32)[None]
    mode_weight = jnp.where(mode_ids < mode_count[0], 1.0 / eigvals, 0.0)

    blocks = sep_map[0]
    outgoing, start_half = operator_rows(
        blocks, (2 * sep_index)[None], mode_weight, gathered, slim
    )
    start_half = start_half.reshape(total_rows // 2, vec_width)
    start_twin = from_twin(start_half)
    incoming = lax.all_to_all(outgoing, "sub", 0, 0, tiled=True)
    map_all = incoming[:, 0, local_dofs : local_dofs + KB].astype(jnp.int32).reshape(-1)

    row_start = core * SB + layer * slim
    flex_rows = lax.dynamic_slice_in_dim(flex, row_start, slim, 0)
    first_rows, own_half, twin_half = build_rows(
        map_all, core[None], incoming, flex_rows, start_half, start_twin
    )
    operator_half = jnp.concatenate([own_half, from_twin(twin_half)], axis=0)

    def from_layer(x, distance):
        perm = [(z * 2 + c, (z ^ distance) * 2 + c) for z in range(layers) for c in range(2)]
        return lax.ppermute(x, "sub", perm)

    def gather_half(rows, after):
        other = from_layer(rows, 4)
        upper = (layer & 4) > 0
        pair = jnp.stack([jnp.where(upper, other, rows), jnp.where(upper, rows, other)])
        pieces = [pair] + [from_layer(pair, distance) for distance in (1, 2, 3)]
        spread = spread_rows((layer & 3)[None], pieces, after, sep_count)
        whole = lax.all_to_all(spread, "sep", 0, 0, tiled=True)
        return whole.reshape(total_rows // 2, vec_width), pieces[1]

    first_half, _ = gather_half(first_rows, operator_half)
    both_rows = dot_f32(operator_half, first_half)
    second_rows = both_rows[:slim] + from_twin(both_rows[slim:])
    raw_half, second_piece = gather_half(second_rows, second_rows)

    first_gram = gram_of(first_half, second_piece)
    first_factor = inverse_transposed_factor(first_gram, from_twin(first_gram), scaling)
    iterate_half = iterate_of(first_half, first_factor)

    twin_blocks = lax.dynamic_slice_in_dim(map_all, (sub_index ^ 1) * KB, KB, 0)
    image_half, picks, second_sums = image_and_sums(
        jnp.concatenate([sep_index[None], twin_blocks >> 1]), raw_half, iterate_half, first_factor
    )
    wanted = jnp.concatenate([2 * sep_index + jnp.arange(2, dtype=jnp.int32), blocks])
    separator_modes, quotient, interior = last_products(
        wanted >> 1,
        ((wanted & 1) == core).astype(jnp.int32),
        second_sums,
        from_twin(second_sums),
        image_half,
        from_twin(picks),
        mode_weight,
        gathered,
        shapes,
        scaling,
    )
    return (separator_modes, quotient[0], interior[None])


def solution(mesh):
    placed = (
        P("sub", "sep", None),
        P("sub", "sep", None),
        P("sub", None),
        P("sub"),
        P("sub", None),
        P("sub", None),
        P("sep", None),
        P("sep", None),
    )
    return jax.shard_map(
        per_device,
        mesh=mesh,
        in_specs=placed,
        out_specs=(P("sep", None), P(), P("sub", "sep", None)),
        check_vma=False,
    )
```

```python
import jax
import jax.numpy as jnp
from jax import lax
from jax.experimental import pallas as pl
from jax.experimental.pallas import tpu as pltpu
from jax.sharding import PartitionSpec as P

KB = 4
SB = 128
CHUNK = 2048
VMEM_BYTES = 20 * 1024 * 1024
HIGHEST = lax.Precision.HIGHEST
WHOLE = pl.BlockSpec(memory_space=pltpu.VMEM)


def dot_f32(a, b, contract=((1,), (0,))):
    return lax.dot_general(
        a, b, (contract, ((), ())), precision=HIGHEST, preferred_element_type=jnp.float32
    )


def split_three(x):
    high = x.astype(jnp.bfloat16)
    rest = x - high.astype(jnp.float32)
    middle = rest.astype(jnp.bfloat16)
    return high, middle, (rest - middle.astype(jnp.float32)).astype(jnp.bfloat16)


def invert_factor(left_ref, right_ref):
    n = left_ref.shape[0]
    subs = lax.broadcasted_iota(jnp.int32, (8, n), 0)
    lanes = lax.broadcasted_iota(jnp.int32, (8, n), 1)

    def spread(x, row, lane):
        return jnp.broadcast_to(x[row : row + 1, lane : lane + 1], (8, n))

    def row_of(x, row):
        return jnp.broadcast_to(x[row : row + 1, :], (8, n))

    def stacked(pieces, base):
        out = base
        for row, piece in pieces:
            out = jnp.where(subs == row, piece, out)
        return out

    def panel(t, carry):
        start = pl.multiple_of(8 * t, 8)
        shift = (n - 8 * t) & (n - 1)
        pivots = left_ref[pl.ds(start, 8), :]
        pivots_right = right_ref[pl.ds(start, 8), :]
        corner = pltpu.roll(pivots, shift, 1)
        a = {(i, j): spread(corner, i, j) for i in range(8) for j in range(i + 1)}
        inverse, m = [], {}
        for j in range(8):
            inverse.append(1.0 / a[j, j])
            for i in range(j + 1, 8):
                m[i, j] = a[i, j] * inverse[j]
            for i in range(j + 1, 8):
                for k in range(j + 1, i + 1):
                    a[i, k] = a[i, k] - m[i, j] * a[k, j]
        unit = {}
        for i in range(8):
            for k in range(i):
                total = -m[i, k]
                for j in range(k + 1, i):
                    total = total - m[i, j] * unit[j, k]
                unit[i, k] = total
        zero = jnp.zeros((8, n), jnp.float32)
        down = [stacked([(i, unit[i, k]) for i in range(k + 1, 8)], zero) for k in range(7)]
        up = [stacked([(k, unit[i, k]) for k in range(i)], zero) for i in range(1, 8)]
        scale = stacked([(i, inverse[i]) for i in range(1, 8)], inverse[0])
        root = stacked([(i, a[i, i]) for i in range(1, 8)], a[0, 0])

        def reduce_rows(x):
            for_out = x
            for k in range(7):
                for_out = for_out + down[k] * row_of(x, k)
            scaled = for_out * scale
            back = scaled
            for i in range(1, 8):
                back = back + up[i - 1] * row_of(scaled, i)
            return for_out, back

        _, back_left = reduce_rows(pivots)
        done_right, back_right = reduce_rows(pivots_right)
        heads = jnp.where(lanes > 8 * t + 7, pivots, 0.0)
        upper = split_three(heads)
        lower = split_three(jnp.concatenate([back_left, back_right], axis=1))
        pairs = ((0, 0), (0, 1), (1, 0), (0, 2), (2, 0), (1, 1))
        change = lax.dot_general(
            jnp.concatenate([upper[p] for p, _ in pairs], axis=0),
            jnp.concatenate([lower[q] for _, q in pairs], axis=0),
            (((0,), (0,)), ((), ())),
            preferred_element_type=jnp.float32,
        )
        left_ref[...] = left_ref[...] - change[:, :n]
        right_ref[...] = right_ref[...] - change[:, n:]
        right_ref[pl.ds(start, 8), :] = done_right * lax.rsqrt(root)
        return carry

    lax.fori_loop(0, n // 8, panel, 0)


def factor_kernel(scale, gram_ref, twin_ref, out_ref, left_ref, right_ref):
    half = gram_ref.shape[1] // 2
    identity = jnp.where(
        lax.broadcasted_iota(jnp.int32, (half, half), 0)
        == lax.broadcasted_iota(jnp.int32, (half, half), 1),
        1.0,
        0.0,
    ).astype(jnp.float32)
    left_ref[...] = gram_ref[:half, :half] + twin_ref[:half, :half]
    right_ref[...] = identity
    invert_factor(left_ref, right_ref)
    first = right_ref[...]
    below = dot_f32(gram_ref[half : 2 * half, :half] + twin_ref[half : 2 * half, :half], first, ((1,), (1,)))
    left_ref[...] = (
        gram_ref[half : 2 * half, half:] + twin_ref[half : 2 * half, half:]
    ) - dot_f32(below, below, ((1,), (1,)))
    right_ref[...] = identity
    invert_factor(left_ref, right_ref)
    second = right_ref[...]
    corner = -dot_f32(second, dot_f32(below, first))
    out_ref[:half, :half] = first.T * scale
    out_ref[:half, half:] = corner.T * scale
    out_ref[half:, :half] = jnp.zeros((half, half), jnp.float32)
    out_ref[half:, half:] = second.T * scale


def inverse_transposed_factor(gram, twin, scale):
    half = gram.shape[0] // 2
    return pl.pallas_call(
        lambda *refs: factor_kernel(scale, *refs),
        out_shape=jax.ShapeDtypeStruct(gram.shape, jnp.float32),
        in_specs=[pl.BlockSpec(memory_space=pltpu.VMEM)] * 2,
        out_specs=pl.BlockSpec(memory_space=pltpu.VMEM),
        scratch_shapes=[pltpu.VMEM((half, half), jnp.float32)] * 2,
        compiler_params=pltpu.CompilerParams(vmem_limit_bytes=VMEM_BYTES),
        cost_estimate=pl.CostEstimate(
            flops=12_000_000_000, bytes_accessed=800_000, transcendentals=256
        ),
        name="factor",
    )(gram, twin)


def gram_step(x, even_ref, odd_ref):
    high, middle, low = split_three(x)

    def product(a, b):
        return lax.dot_general(
            a, b, (((0,), (0,)), ((), ())), preferred_element_type=jnp.float32
        )

    even_ref[...] += product(high, high) + product(middle, middle)
    odd_ref[...] += product(high, middle) + product(high, low)


def gram_kernel(x_ref, after_ref, out_ref, even_ref, odd_ref):
    even_ref[...] = jnp.zeros_like(even_ref)
    odd_ref[...] = jnp.zeros_like(odd_ref)

    def chunk(c, carry):
        gram_step(x_ref[pl.ds(pl.multiple_of(c * CHUNK, CHUNK), CHUNK), :], even_ref, odd_ref)
        return carry

    lax.fori_loop(0, x_ref.shape[0] // CHUNK, chunk, 0)
    out_ref[...] = even_ref[...] + odd_ref[...] + odd_ref[...].T


def gram_of(x, after):
    width = x.shape[1]
    return pl.pallas_call(
        gram_kernel,
        out_shape=jax.ShapeDtypeStruct((width, width), jnp.float32),
        in_specs=[WHOLE, pl.BlockSpec(memory_space=pl.ANY)],
        out_specs=WHOLE,
        scratch_shapes=[pltpu.VMEM((width, width), jnp.float32)] * 2,
        compiler_params=pltpu.CompilerParams(vmem_limit_bytes=VMEM_BYTES),
        cost_estimate=pl.CostEstimate(
            flops=2_000_000_000, bytes_accessed=2_400_000, transcendentals=0
        ),
        name="gram",
    )(x, after)


def iterate_kernel(first_ref, factor_ref, iterate_ref, local_ref, sem):
    local_ref[...] = dot_f32(first_ref[...], factor_ref[...])
    store = pltpu.make_async_copy(local_ref, iterate_ref, sem)
    store.start()
    store.wait()


def iterate_of(first, factor):
    return pl.pallas_call(
        iterate_kernel,
        out_shape=jax.ShapeDtypeStruct(first.shape, jnp.float32),
        in_specs=[WHOLE, WHOLE],
        out_specs=pl.BlockSpec(memory_space=pl.ANY),
        scratch_shapes=[pltpu.VMEM(first.shape, jnp.float32), pltpu.SemaphoreType.DMA],
        compiler_params=pltpu.CompilerParams(vmem_limit_bytes=VMEM_BYTES),
        cost_estimate=pl.CostEstimate(
            flops=2_000_000_000, bytes_accessed=4_000_000, transcendentals=0
        ),
        name="iterate",
    )(first, factor)


def image_kernel(
    place_ref, raw_ref, iterate_ref, factor_ref, image_ref, picks_ref, out_ref, even_ref, odd_ref,
    local_ref, sem,
):
    load = pltpu.make_async_copy(iterate_ref, local_ref, sem)
    load.start()
    width = even_ref.shape[0]
    even_ref[...] = jnp.zeros_like(even_ref)
    odd_ref[...] = jnp.zeros_like(odd_ref)
    image = dot_f32(raw_ref[...], factor_ref[...])
    image_ref[...] = image
    for k in range(1 + KB):
        source = pl.ds(pl.multiple_of(place_ref[k] * SB, SB), SB)
        picks_ref[k * SB : (k + 1) * SB, :] = image_ref[source, :]
    gram_step(image, even_ref, odd_ref)
    load.wait()
    iterate = local_ref[...]
    out_ref[width:, :] = jnp.zeros((out_ref.shape[0] - width, width), jnp.float32)
    out_ref[width : width + 1, :] = jnp.sum(iterate * image, axis=0, keepdims=True)
    out_ref[width + 1 : width + 2, :] = jnp.sum(iterate * iterate, axis=0, keepdims=True)
    out_ref[:width, :] = even_ref[...] + odd_ref[...] + odd_ref[...].T


def image_and_sums(place, raw, iterate, factor):
    rows, width = raw.shape
    return pl.pallas_call(
        image_kernel,
        out_shape=(
            jax.ShapeDtypeStruct((rows, width), jnp.float32),
            jax.ShapeDtypeStruct(((1 + KB) * SB, width), jnp.float32),
            jax.ShapeDtypeStruct((width + 8, width), jnp.float32),
        ),
        in_specs=[
            pl.BlockSpec(memory_space=pltpu.SMEM),
            WHOLE,
            pl.BlockSpec(memory_space=pl.ANY),
            WHOLE,
        ],
        out_specs=(WHOLE, WHOLE, WHOLE),
        scratch_shapes=[pltpu.VMEM((width, width), jnp.float32)] * 2
        + [pltpu.VMEM((rows, width), jnp.float32), pltpu.SemaphoreType.DMA],
        compiler_params=pltpu.CompilerParams(vmem_limit_bytes=VMEM_BYTES),
        cost_estimate=pl.CostEstimate(
            flops=3_000_000_000, bytes_accessed=7_000_000, transcendentals=0
        ),
        name="image",
    )(place, raw, iterate, factor)


def spread_kernel(low_ref, own_ref, one_ref, two_ref, three_ref, after_ref, out_ref, part_ref, sems):
    slim = own_ref.shape[1]
    for e, piece_ref in enumerate((own_ref, one_ref, two_ref, three_ref)):
        for b in range(2):
            place = (4 * b + (low_ref[0] ^ e)) * slim
            part_ref[pl.ds(pl.multiple_of(place, slim), slim), :] = piece_ref[b]
    copies = [
        pltpu.make_async_copy(part_ref, out_ref.at[k], sems.at[k]) for k in range(out_ref.shape[0])
    ]
    for copy in copies:
        copy.start()
    for copy in copies:
        copy.wait()


def spread_rows(low, pieces, after, count):
    slim, width = pieces[0].shape[1:]
    anywhere = pl.BlockSpec(memory_space=pl.ANY)
    return pl.pallas_call(
        spread_kernel,
        out_shape=jax.ShapeDtypeStruct((count, 8 * slim, width), jnp.float32),
        in_specs=[pl.BlockSpec(memory_space=pltpu.SMEM)] + [WHOLE] * 4 + [anywhere],
        out_specs=anywhere,
        scratch_shapes=[
            pltpu.VMEM((8 * slim, width), jnp.float32),
            pltpu.SemaphoreType.DMA((count,)),
        ],
        cost_estimate=pl.CostEstimate(flops=0, bytes_accessed=2_400_000, transcendentals=0),
        name="spread",
    )(low, *pieces, after)


def rows_kernel(blocks_ref, first_ref, weight_ref, gathered_ref, out_ref, start_ref):
    slim = out_ref.shape[1]
    sources, height, modes = gathered_ref.shape
    height = height // 2
    dofs = sources * height
    width = start_ref.shape[2]
    for q in range(modes // width):
        start_ref[:, height * q : height * (q + 1), :] = gathered_ref[
            :, height:, width * q : width * (q + 1)
        ]
    everything = gathered_ref[:, :height, :].reshape(dofs, modes)
    lane = lax.broadcasted_iota(jnp.int32, (slim, SB), 1)
    numbers = jnp.zeros((slim, SB), jnp.int32)
    for k in range(KB):
        numbers = jnp.where(lane == k, blocks_ref[k], numbers)
    numbers = numbers.astype(jnp.float32).astype(jnp.bfloat16)
    for h in range(2):
        wanted = first_ref[0] + h
        place = jnp.int32(0)
        found = jnp.int32(0)
        for k in range(KB):
            hit = (blocks_ref[k] == wanted).astype(jnp.int32)
            place += k * hit
            found += hit
        span = sources // KB
        picked = gathered_ref[pl.ds(place * span, span), :height, :].reshape(SB, modes)
        weighted = picked.astype(jnp.float32) * (weight_ref[...] * found.astype(jnp.float32))
        high, middle, low = split_three(weighted)

        def product(part):
            return lax.dot_general(
                part, everything, (((1,), (1,)), ((), ())), preferred_element_type=jnp.float32
            )

        rows = (product(high) + (product(middle) + product(low))).astype(jnp.bfloat16)
        for z in range(SB // slim):
            out_ref[2 * z + h, :, :dofs] = rows[z * slim : (z + 1) * slim, :]
            out_ref[2 * z + h, :, dofs:] = numbers


def operator_rows(blocks, first, weight, gathered, slim):
    sources, height, modes = gathered.shape
    dofs = sources * height // 2
    width = height * modes // 2 // SB
    scalars = pl.BlockSpec(memory_space=pltpu.SMEM)
    return pl.pallas_call(
        rows_kernel,
        out_shape=(
            jax.ShapeDtypeStruct((2 * SB // slim, slim, dofs + SB), jnp.bfloat16),
            jax.ShapeDtypeStruct((sources, SB, width), jnp.bfloat16),
        ),
        in_specs=[scalars, scalars, WHOLE, WHOLE],
        out_specs=(WHOLE, WHOLE),
        compiler_params=pltpu.CompilerParams(vmem_limit_bytes=VMEM_BYTES),
        cost_estimate=pl.CostEstimate(
            flops=800_000_000, bytes_accessed=2_700_000, transcendentals=0
        ),
        name="rows",
    )(blocks, first, weight, gathered)


def build_kernel(
    map_ref, core_ref, incoming_ref, flex_ref, start_ref, twin_ref,
    rows_ref, own_ref, other_ref, halves_ref,
):
    slim, total = flex_ref.shape
    for b in range(total // SB):
        halves_ref[b % 2, :, (b // 2) * SB : (b // 2 + 1) * SB] = flex_ref[
            :, b * SB : (b + 1) * SB
        ]
    for s in range(incoming_ref.shape[0]):
        for k in range(KB):
            b = map_ref[s * KB + k]
            place = pl.ds(pl.multiple_of((b >> 1) * SB, SB), SB)
            halves_ref[b & 1, :, place] += incoming_ref[s, :, k * SB : (k + 1) * SB].astype(
                jnp.float32
            )
    own = halves_ref[core_ref[0]]
    other = halves_ref[1 - core_ref[0]]
    own_ref[...] = own
    other_ref[...] = other
    first = jnp.dot(
        jnp.concatenate(split_three(own), axis=0), start_ref[...], preferred_element_type=jnp.float32
    )
    second = jnp.dot(
        jnp.concatenate(split_three(other), axis=0), twin_ref[...], preferred_element_type=jnp.float32
    )
    both = first + second
    rows_ref[...] = both[:slim] + (both[slim : 2 * slim] + both[2 * slim :])


def build_rows(map_all, core, incoming, flex, start, twin):
    slim = incoming.shape[1]
    total = flex.shape[1]
    width = start.shape[1]
    scalars = pl.BlockSpec(memory_space=pltpu.SMEM)
    half = jax.ShapeDtypeStruct((slim, total // 2), jnp.float32)
    return pl.pallas_call(
        build_kernel,
        out_shape=(jax.ShapeDtypeStruct((slim, width), jnp.float32), half, half),
        in_specs=[scalars] * 2 + [WHOLE] * 4,
        out_specs=(WHOLE, WHOLE, WHOLE),
        scratch_shapes=[
            pltpu.VMEM((2, slim, total // 2), jnp.float32),
        ],
        compiler_params=pltpu.CompilerParams(vmem_limit_bytes=VMEM_BYTES),
        cost_estimate=pl.CostEstimate(
            flops=300_000_000, bytes_accessed=4_000_000, transcendentals=0
        ),
        name="build",
    )(map_all, core, incoming, flex, start, twin)


def last_kernel(
    scale,
    place_ref, here_ref, gram_ref, gram_twin_ref, mine_ref, twin_ref, weight_ref, gathered_ref,
    modes_ref, own_ref, quotient_ref, interior_ref, factor_ref, left_ref, right_ref, image_ref, dofs_ref,
    local_ref, result_ref, image_sems, mode_sem, dofs_sem, result_sems,
):
    count = 2 + KB
    rows = local_ref.shape[0]
    step = rows // 4
    load_modes = pltpu.make_async_copy(modes_ref, local_ref, mode_sem)
    load_dofs = pltpu.make_async_copy(
        gathered_ref.at[:, pl.ds(0, dofs_ref.shape[1]), :], dofs_ref, dofs_sem
    )
    for k in range(count):
        source = pl.ds(pl.multiple_of(place_ref[k] * SB, SB), SB)
        target = image_ref.at[pl.ds(k * SB, SB), :]

        @pl.when(here_ref[k] == 1)
        def _():
            pltpu.make_async_copy(mine_ref.at[source, :], target, image_sems.at[k]).start()

        @pl.when(here_ref[k] != 1)
        def _():
            picked = pl.ds((0 if k < 2 else k - 1) * SB, SB)
            pltpu.make_async_copy(twin_ref.at[picked, :], target, image_sems.at[k]).start()

    load_modes.start()
    load_dofs.start()
    width = gram_ref.shape[1]
    sums = gram_ref[width:, :] + gram_twin_ref[width:, :]
    quotient_ref[...] = sums[0:1, :] / sums[1:2, :]
    factor_kernel(scale, gram_ref, gram_twin_ref, factor_ref, left_ref, right_ref)
    for k in range(count):
        target = image_ref.at[pl.ds(k * SB, SB), :]
        pltpu.make_async_copy(mine_ref.at[pl.ds(0, SB), :], target, image_sems.at[k]).wait()
    load_dofs.wait()
    load_modes.wait()
    vectors = dot_f32(image_ref[...], factor_ref[...])
    own_ref[...] = vectors[: 2 * SB, :]
    touched = vectors[2 * SB :, :].astype(jnp.bfloat16)
    amplitude = lax.dot_general(
        touched,
        dofs_ref[...].reshape(KB * SB, dofs_ref.shape[2]),
        (((0,), (0,)), ((), ())),
        preferred_element_type=jnp.float32,
    )
    terms = (weight_ref[...] * amplitude).astype(jnp.bfloat16)
    stores = []
    for c in range(4):
        part = pl.ds(c * step, step)
        result_ref[part, :] = lax.dot_general(
            local_ref[part, :], terms, (((1,), (1,)), ((), ())), preferred_element_type=jnp.float32
        ).astype(jnp.bfloat16)
        stores.append(
            pltpu.make_async_copy(result_ref.at[part, :], interior_ref.at[part, :], result_sems.at[c])
        )
        stores[-1].start()
    for store in stores:
        store.wait()


def last_products(place, here, gram, gram_twin, mine, twin, weight, gathered, modes, scale):
    width = gram.shape[1]
    rows, count = modes.shape
    scalars = pl.BlockSpec(memory_space=pltpu.SMEM)
    anywhere = pl.BlockSpec(memory_space=pl.ANY)
    return pl.pallas_call(
        lambda *refs: last_kernel(scale, *refs),
        in_specs=[scalars, scalars, WHOLE, WHOLE, anywhere, anywhere, WHOLE, anywhere, anywhere],
        out_specs=(WHOLE, WHOLE, anywhere),
        out_shape=(
            jax.ShapeDtypeStruct((2 * SB, width), jnp.float32),
            jax.ShapeDtypeStruct((1, width), jnp.float32),
            jax.ShapeDtypeStruct((rows, width), jnp.bfloat16),
        ),
        scratch_shapes=[
            pltpu.VMEM((width, width), jnp.float32),
            pltpu.VMEM((width // 2, width // 2), jnp.float32),
            pltpu.VMEM((width // 2, width // 2), jnp.float32),
            pltpu.VMEM(((2 + KB) * SB, width), jnp.float32),
            pltpu.VMEM((gathered.shape[0], gathered.shape[1] // 2, count), jnp.bfloat16),
            pltpu.VMEM((rows, count), jnp.bfloat16),
            pltpu.VMEM((rows, width), jnp.bfloat16),
            pltpu.SemaphoreType.DMA((2 + KB,)),
            pltpu.SemaphoreType.DMA,
            pltpu.SemaphoreType.DMA,
            pltpu.SemaphoreType.DMA((4,)),
        ],
        compiler_params=pltpu.CompilerParams(vmem_limit_bytes=VMEM_BYTES),
        cost_estimate=pl.CostEstimate(
            flops=16_000_000_000, bytes_accessed=8_000_000, transcendentals=256
        ),
        name="last",
    )(place, here, gram, gram_twin, mine, twin, weight, gathered, modes)


def gather_blocks(x, axis):
    count = lax.axis_size(axis)
    spread = jnp.broadcast_to(x[None], (count,) + x.shape)
    return lax.all_to_all(spread, axis, 0, 0, tiled=True)


def per_device(modes, coupling, eigvals, mode_count, sep_map, sep_len, flex, init_vectors):
    shapes = modes[0]
    sep_count = lax.axis_size("sep")
    sub_count = lax.axis_size("sub")
    sep_index = lax.axis_index("sep")
    sub_index = lax.axis_index("sub")
    layers = sub_count // 2
    layer, core = sub_index >> 1, sub_index & 1
    mode_total = shapes.shape[1]
    vec_width = init_vectors.shape[1]
    owned_rows = init_vectors.shape[0]
    total_rows = owned_rows * sep_count
    local_dofs = KB * SB
    slim = SB // layers
    scaling = float(total_rows) ** 0.5

    def from_twin(x):
        return lax.ppermute(x, "sub", [(i, i ^ 1) for i in range(sub_count)])

    share = local_dofs // sep_count
    partial = lax.dot_general(
        coupling[0], shapes, (((0,), (0,)), ((), ())), preferred_element_type=jnp.float32
    )
    partial = partial.astype(jnp.bfloat16)
    shares = lax.all_to_all(
        partial.reshape(sep_count, share, mode_total), "sep", 0, 0, tiled=True
    )
    first_dof = sep_index * share
    length = lax.dynamic_index_in_dim(sep_len[0], first_dof // SB, 0, keepdims=False)
    live = first_dof % SB + jnp.arange(share, dtype=jnp.int32) < length
    own_projected = jnp.sum(shares.astype(jnp.float32), axis=0)
    own_projected = jnp.where(live[:, None], own_projected, 0.0).astype(jnp.bfloat16)
    fold = mode_total // vec_width
    start_rows = lax.dynamic_slice_in_dim(init_vectors, core * SB, SB, 0).astype(jnp.bfloat16)
    start_rows = jnp.concatenate([start_rows[share * q : share * (q + 1)] for q in range(fold)], axis=1)
    gathered = gather_blocks(jnp.concatenate([own_projected, start_rows], axis=0), "sep")
    mode_ids = jnp.arange(mode_total, dtype=jnp.int32)[None]
    mode_weight = jnp.where(mode_ids < mode_count[0], 1.0 / eigvals, 0.0)

    blocks = sep_map[0]
    outgoing, start_half = operator_rows(
        blocks, (2 * sep_index)[None], mode_weight, gathered, slim
    )
    start_half = start_half.reshape(total_rows // 2, vec_width)
    start_twin = from_twin(start_half)
    incoming = lax.all_to_all(outgoing, "sub", 0, 0, tiled=True)
    map_all = incoming[:, 0, local_dofs : local_dofs + KB].astype(jnp.int32).reshape(-1)

    row_start = core * SB + layer * slim
    flex_rows = lax.dynamic_slice_in_dim(flex, row_start, slim, 0)
    first_rows, own_half, twin_half = build_rows(
        map_all, core[None], incoming, flex_rows, start_half, start_twin
    )
    operator_half = jnp.concatenate([own_half, from_twin(twin_half)], axis=0)

    def from_layer(x, distance):
        perm = [(z * 2 + c, (z ^ distance) * 2 + c) for z in range(layers) for c in range(2)]
        return lax.ppermute(x, "sub", perm)

    def gather_half(rows, after):
        other = from_layer(rows, 4)
        upper = (layer & 4) > 0
        pair = jnp.stack([jnp.where(upper, other, rows), jnp.where(upper, rows, other)])
        pieces = [pair] + [from_layer(pair, distance) for distance in (1, 2, 3)]
        spread = spread_rows((layer & 3)[None], pieces, after, sep_count)
        whole = lax.all_to_all(spread, "sep", 0, 0, tiled=True)
        return whole.reshape(total_rows // 2, vec_width), spread

    first_half, _ = gather_half(first_rows, operator_half)
    both_rows = dot_f32(operator_half, first_half)
    second_rows = both_rows[:slim] + from_twin(both_rows[slim:])
    raw_half, second_spread = gather_half(second_rows, second_rows)

    first_gram = gram_of(first_half, second_spread)
    first_factor = inverse_transposed_factor(first_gram, from_twin(first_gram), scaling)
    iterate_half = iterate_of(first_half, first_factor)

    twin_blocks = lax.dynamic_slice_in_dim(map_all, (sub_index ^ 1) * KB, KB, 0)
    image_half, picks, second_sums = image_and_sums(
        jnp.concatenate([sep_index[None], twin_blocks >> 1]), raw_half, iterate_half, first_factor
    )
    wanted = jnp.concatenate([2 * sep_index + jnp.arange(2, dtype=jnp.int32), blocks])
    separator_modes, quotient, interior = last_products(
        wanted >> 1,
        ((wanted & 1) == core).astype(jnp.int32),
        second_sums,
        from_twin(second_sums),
        image_half,
        from_twin(picks),
        mode_weight,
        gathered,
        shapes,
        scaling,
    )
    return (separator_modes, quotient[0], interior[None])


def solution(mesh):
    placed = (
        P("sub", "sep", None),
        P("sub", "sep", None),
        P("sub", None),
        P("sub"),
        P("sub", None),
        P("sub", None),
        P("sep", None),
        P("sep", None),
    )
    return jax.shard_map(
        per_device,
        mesh=mesh,
        in_specs=placed,
        out_specs=(P("sep", None), P(), P("sub", "sep", None)),
        check_vma=False,
    )
```
